32 devices in a mesh: rows: 8 (over z, core), cols: 4 (over y, x).
Axes of the slice: x: 2, y: 2, z: 4, core: 2. Of those that a mesh axis runs over, the one named last changes fastest.
Arguments:
- scalar: float32 [16, 256, 2048], P(None, 'rows', 'cols'), may hold values from -6 to 6
- diffusivity: float32 [16, 256, 2048], P(None, 'rows', 'cols'), may hold values from 0.05 to 0.5
- vel_modes: float32 [6, 32, 256], P(None, 'rows', 'cols'), may hold values from -8 to 8
- offsets: int32 [256], P('rows'), may hold values from -1 to 1
Outputs:
- advanced: float32 [16, 256, 2048], P(None, 'rows', 'cols')
The draws below stay inside these ranges and needn't reach their ends.
All inputs are finite; a program needn't handle non-finite values.
Results may differ from the reference program's by a relative error of at most 0.00007.
Values sent between devices are 32-bit elements; how exact they have to be, the bound alone decides.
A program may use at most 64 MiB of HBM per device.

```python
import math
import jax
import jax.numpy as jnp
from jax import lax

PL = 16
NX = 256
NY = 2048
NXC = 32
NYC = 256
CZP = 3


def draw_vel_modes(key, part):
    extent = (2 * CZP, NXC, NYC)
    rough_key = jax.random.fold_in(key, 11)
    values = jax.random.truncated_normal(rough_key, -4.0, 4.0, extent, jnp.float32) * (3.5 / NYC ** 0.5)
    return jnp.clip(values, -8.0, 8.0)


def set_ends(values, own_key, least, high):
    shape = values.shape
    place = [jax.random.randint(jax.random.fold_in(own_key, axis), (), 0, shape[axis]) for axis in range(len(shape))]
    values = values.at[tuple(place)].set(least)
    longest = shape.index(max(shape))
    place[longest] = (place[longest] + 1) % shape[longest]
    return values.at[tuple(place)].set(high)


def level_of(key, shape, pieces, low, largest):
    def one(axis_at, shards_of):
        heights = jax.random.uniform(jax.random.fold_in(jax.random.fold_in(key, 6), axis_at), (shards_of,), jnp.float32, low / len(pieces), largest / len(pieces))
        return jnp.repeat(jnp.exp(heights), shape[axis_at] // shards_of).reshape((-1,) + (1,) * (len(shape) - axis_at - 1))

    gain = one(*pieces[0])
    for cut in pieces[1:]:
        gain = gain * one(*cut)
    return gain


def noise(rng, shape, width, most, cuts=(), kind=jnp.bfloat16):
    result = jax.random.normal(rng, shape, jnp.float32) * width
    if len(cuts) > 0:
        result = level_of(rng, shape, cuts, -0.22, 0.18) * result
    return jnp.clip(result, min=-most, max=most).astype(kind)


def setup_inputs(seed: int = 0) -> dict:
    key_of = jax.random.split(jax.random.key(seed), 5)
    return {
        "scalar": noise(key_of[0], (PL, NX, NY), 1.0, 6.0, ((1, 8), (2, 4)), jnp.float32),
        "diffusivity": jnp.clip(jnp.exp(math.log(0.5) - 2.3025851 * jax.random.uniform(key_of[1], (PL, NX, NY), jnp.float32) ** level_of(key_of[1], (PL, NX, NY), ((1, 8), (2, 4)), -0.2, 0.2)), 0.05, 0.5),
        "vel_modes": draw_vel_modes(jax.random.fold_in(key_of[4], 71), 0),
        "offsets": set_ends(jax.random.randint(key_of[3], (NX,), -1, 2), jax.random.fold_in(key_of[3], 1), -1, 1).astype(jnp.int32),
    }


time_step = 0.25


def window(source, row_step, col_step):
    height = source.shape[1]
    breadth = source.shape[2]
    return source[:, 2 + row_step:height - 2 + row_step, 2 + col_step:breadth - 2 + col_step]


def tendency(field, speed_rows, speed_cols, kappa):
    centre = window(field, 0, 0)
    slope_rows = (8.0 * (window(field, 1, 0) - window(field, -1, 0)) - (window(field, 2, 0) - window(field, -2, 0))) / 12.0
    slope_cols = (8.0 * (window(field, 0, 1) - window(field, 0, -1)) - (window(field, 0, 2) - window(field, 0, -2))) / 12.0
    kappa_centre = window(kappa, 0, 0)
    flux_east = 0.5 * (kappa_centre + window(kappa, 1, 0)) * (window(field, 1, 0) - centre)
    flux_west = 0.5 * (kappa_centre + window(kappa, -1, 0)) * (centre - window(field, -1, 0))
    flux_north = 0.5 * (kappa_centre + window(kappa, 0, 1)) * (window(field, 0, 1) - centre)
    flux_south = 0.5 * (kappa_centre + window(kappa, 0, -1)) * (centre - window(field, 0, -1))
    return (flux_east - flux_west) + (flux_north - flux_south) - (window(speed_rows, 0, 0) * slope_rows + window(speed_cols, 0, 0) * slope_cols)


def padded_zero(source):
    return jnp.pad(source, ((0, 0), (2, 2), (2, 2)))


def runge_kutta(field, speed_rows, speed_cols, kappa_ext, extend):
    speed_rows = padded_zero(speed_rows)
    speed_cols = padded_zero(speed_cols)
    first = tendency(extend(field), speed_rows, speed_cols, kappa_ext)
    second = tendency(extend(field + 0.5 * time_step * first), speed_rows, speed_cols, kappa_ext)
    third = tendency(extend(field + 0.5 * time_step * second), speed_rows, speed_cols, kappa_ext)
    fourth = tendency(extend(field + time_step * third), speed_rows, speed_cols, kappa_ext)
    return field + (time_step / 6.0) * (first + 2.0 * second + 2.0 * third + fourth)


def hartley_table(wavenum, places, length):
    product = (wavenum[:, None] * places[None, :]) % length
    angle = product.astype(jnp.float32) * (2.0 * jnp.pi / length)
    return jnp.cos(angle) + jnp.sin(angle)


def blend_weights(base, fraction, count):
    places = jnp.arange(count, dtype=jnp.int32)
    lower = (places[None, :] == base[:, None]).astype(jnp.float32)
    upper = (places[None, :] == ((base + 1) % count)[:, None]).astype(jnp.float32)
    return (1.0 - fraction)[:, None] * lower + fraction[:, None] * upper


def wrapped(source):
    return jnp.pad(source, ((0, 0), (2, 2), (2, 2)), mode="wrap")


def reference(scalar, diffusivity, vel_modes, offsets):
    highest = lax.Precision.HIGHEST
    coarse_planes = vel_modes.shape[0] // 2
    coarse_rows = vel_modes.shape[1]
    length = vel_modes.shape[2]
    wavenum = jnp.arange(length, dtype=jnp.int32)
    physical = jnp.einsum("cak,kb->cab", vel_modes, hartley_table(wavenum, wavenum, length), precision=highest)
    fine_rows = jnp.arange(scalar.shape[1], dtype=jnp.int32)
    row_blend = blend_weights((fine_rows // 8 + offsets) % coarse_rows, (fine_rows % 8).astype(jnp.float32) / 8.0, coarse_rows)
    fine_cols = jnp.arange(scalar.shape[2], dtype=jnp.int32)
    col_blend = blend_weights(fine_cols // 8, (fine_cols % 8).astype(jnp.float32) / 8.0, length)
    fine_planes = jnp.arange(scalar.shape[0], dtype=jnp.int32)
    plane_blend = blend_weights(fine_planes // 8, (fine_planes % 8).astype(jnp.float32) / 8.0, coarse_planes)
    along = jnp.einsum("cab,jb->caj", physical, col_blend, precision=highest)
    across = jnp.einsum("ia,caj->cij", row_blend, along, precision=highest)
    across = across.reshape(2, coarse_planes, scalar.shape[1], scalar.shape[2])

    def one_plane(items):
        field, kappa, weights = items
        speeds = jnp.einsum("q,mqij->mij", weights, across, precision=highest)
        return runge_kutta(field[None], speeds[0][None], speeds[1][None], wrapped(kappa[None]), wrapped)[0]

    return lax.map(one_plane, (scalar, diffusivity, plane_blend))
```

```python
import functools

import jax
import jax.numpy as jnp
import ml_dtypes
import numpy as np
from jax import lax
from jax.experimental import pallas as pl
from jax.experimental.pallas import tpu as pltpu
from jax.sharding import PartitionSpec as P

TIME_STEP = 0.25
RATIO = 8
HALO = 8
LANES = 128
SUB = 8
MESH = pl.DeviceIdType.MESH
HIGHEST = lax.Precision.HIGHEST


def tables(count, modes_dev, cols_dev, planes, coarse_planes, coarse_rows):
    length = count * modes_dev
    coarse_cols = cols_dev // RATIO
    tiles = cols_dev // LANES + 1
    width = tiles * LANES

    def turn(product):
        return 2.0 * np.pi * (product % length) / length

    wavenum = np.arange(length).reshape(count, modes_dev)
    first = turn(np.arange(count)[:, None, None] * coarse_cols * wavenum[None])
    shift = np.concatenate([np.cos(first) + np.sin(first), np.cos(first) - np.sin(first)], axis=-1)
    shift = shift * (0.5 * TIME_STEP / 12.0)
    places = np.arange(coarse_cols + 3) - 1
    local = turn(wavenum[:, :, None] * places[None, None, :])
    local = np.concatenate([np.cos(local), np.sin(local)], axis=1).reshape(2 * length, -1)
    breadth = -(-local.shape[1] // LANES) * LANES
    transform = np.zeros((2 * length, breadth))
    transform[:, : local.shape[1]] = local
    lane = np.arange(width)
    fine = np.where(lane >= width - HALO, lane - width, np.minimum(lane, cols_dev + HALO - 1))
    col_blend = np.zeros((breadth, width))
    base = fine // RATIO + 1
    share = (fine % RATIO) / RATIO
    col_blend[base, lane] += 1.0 - share
    col_blend[base + 1, lane] += share
    group = -(-coarse_planes * coarse_rows // 16) * 16
    depth = -(-9 * group // LANES) * LANES
    plane_blend = np.zeros((planes, depth))
    row_of = np.full((SUB, depth), -100.0)
    plane = np.arange(planes)
    weights = np.zeros((planes, coarse_planes))
    for p in plane:
        weights[p, p // RATIO % coarse_planes] += 1.0 - (p % RATIO) / RATIO
        weights[p, (p // RATIO + 1) % coarse_planes] += (p % RATIO) / RATIO
    for part in range(3):
        for block in range(3):
            for q in range(coarse_planes):
                for a in range(coarse_rows):
                    at = (part * 3 + block) * group + q * coarse_rows + a
                    plane_blend[:, at] = weights[:, q]
                    row_of[:, at] = block * coarse_rows + a
    as_f32 = functools.partial(np.asarray, dtype=np.float32)
    return (
        as_f32(shift),
        as_f32(transform),
        np.asarray(col_blend, ml_dtypes.bfloat16),
        as_f32(plane_blend),
        as_f32(row_of),
    )


def parts_of(value):
    high = value.astype(jnp.bfloat16)
    rest = value - high.astype(jnp.float32)
    middle = rest.astype(jnp.bfloat16)
    low = (rest - middle.astype(jnp.float32)).astype(jnp.bfloat16)
    return high, middle, low


def kernel(
    n_rows, n_cols, chunks,
    s_ref, k_ref, m_ref, off_ref, shift_ref, transform_ref, blend_ref, planes_ref, rowof_ref,
    o_ref,
    message, modes, packed, strips, above, below, blend_rows, speeds,
    field, kappa, state_b, state_c, state_d, coef,
    vel_send, vel_recv, strip_send, strip_recv, row_send, row_recv,
):
    planes, rows_dev, cols_dev = s_ref.shape
    own_tiles = cols_dev // LANES
    tiles = own_tiles + 1
    tall = rows_dev + 2 * HALO
    coarse = m_ref.shape[0]
    coarse_planes = coarse // 2
    coarse_rows = m_ref.shape[1]
    group = modes.shape[1] // 3 // 2 - SUB // 2
    block = 2 * group + SUB
    r = lax.axis_index("rows")
    c = lax.axis_index("cols")
    row_at = {-1: lax.rem(r + n_rows - 1, n_rows), 0: r, 1: lax.rem(r + 1, n_rows)}
    col_at = [c] + [lax.rem(c + d, n_cols) for d in range(1, n_cols)]
    left, right = col_at[n_cols - 1], col_at[1]

    barrier = pltpu.get_barrier_semaphore()
    partners = [(dr, d) for d in range(n_cols) for dr in (-1, 0, 1) if (dr, d) != (0, 0)]
    for dr, d in partners:
        pl.semaphore_signal(barrier, inc=1, device_id=(row_at[dr], col_at[d]), device_id_type=MESH)

    message[...] = jnp.zeros_like(message)
    for part in range(coarse):
        at = part // coarse_planes * group + part % coarse_planes * coarse_rows
        once = m_ref[part]
        message[at : at + coarse_rows, :] = jnp.concatenate([once, once], axis=-1)
    message[2 * group :, 0:rows_dev] = jnp.broadcast_to(
        off_ref[...].astype(jnp.float32), (SUB, rows_dev)
    )
    pl.semaphore_wait(barrier, len(partners))

    def send(src, dst, sems, target):
        copy = pltpu.make_async_remote_copy(
            src_ref=src, dst_ref=dst, send_sem=sems[0], recv_sem=sems[1],
            device_id=target, device_id_type=MESH,
        )
        copy.start()
        return copy

    vel_copies = []
    for index, (dr, d) in enumerate(partners):
        vel_copies.append(send(
            message, modes.at[c, pl.ds((1 - dr) * block, block)],
            (vel_send.at[index], vel_recv.at[index]), (row_at[dr], col_at[d]),
        ))

    lane8 = lax.broadcasted_iota(jnp.int32, (rows_dev, LANES), 1)
    for side in range(2):
        for array, ref in enumerate((s_ref, k_ref)):
            total = jnp.zeros((rows_dev, LANES), jnp.float32)
            for p in range(planes):
                if side == 0:
                    edge = pltpu.roll(ref[p, :, 0:LANES], (HALO * p) % LANES, 1)
                else:
                    edge = pltpu.roll(ref[p, :, cols_dev - LANES :], (HALO * (p + 1)) % LANES, 1)
                total = jnp.where(lane8 // HALO == p, edge, total)
            packed[side, array] = total
    strip_copies = []
    for side, target in ((0, left), (1, right)):
        there = strips.at[1 - side]
        for index, (dr, first, extent, place) in enumerate((
            (0, 0, rows_dev, HALO),
            (-1, 0, HALO, HALO + rows_dev),
            (1, rows_dev - HALO, HALO, 0),
        )):
            at = side * 3 + index
            strip_copies.append(send(
                packed.at[side, :, pl.ds(first, extent)], there.at[:, pl.ds(place, extent)],
                (strip_send.at[at], strip_recv.at[at]), (row_at[dr], target),
            ))

    per_chunk = planes // chunks
    row_copies = []
    for chunk in range(chunks):
        mine = pl.ds(chunk * per_chunk, per_chunk)
        held = []
        for array, ref in enumerate((s_ref, k_ref)):
            at = (chunk * 2 + array) * 2
            held.append(send(
                ref.at[mine, pl.ds(0, HALO)], below.at[array, mine],
                (row_send.at[at], row_recv.at[at]), (row_at[-1], c),
            ))
            held.append(send(
                ref.at[mine, pl.ds(rows_dev - HALO, HALO)], above.at[array, mine],
                (row_send.at[at + 1], row_recv.at[at + 1]), (row_at[1], c),
            ))
        row_copies.append(held)

    modes[c, pl.ds(block, block)] = message[...]
    for copy in vel_copies:
        copy.wait_recv()
    depth = rowof_ref.shape[1]
    offsets_at = jnp.zeros((tall, LANES), jnp.float32)
    lane = lax.broadcasted_iota(jnp.int32, (tall, LANES), 1)
    ext = lax.broadcasted_iota(jnp.int32, (tall, LANES), 0)
    for part in range(3):
        values = modes[c, part * block + 2 * group : (part + 1) * block, :][0:1]
        here = (lane == ext - HALO + rows_dev * (1 - part)) & (lane < rows_dev)
        offsets_at = offsets_at + jnp.where(here, values, 0.0)
    offset = jnp.dot(
        offsets_at, jnp.ones((LANES, depth), jnp.float32), precision=HIGHEST,
        preferred_element_type=jnp.float32,
    )
    fine = lax.broadcasted_iota(jnp.int32, (tall, depth), 0)
    base = (fine // RATIO + (coarse_rows - 1)).astype(jnp.float32) + offset
    share = (fine % RATIO).astype(jnp.float32) / RATIO
    row_of = rowof_ref[0:1, :]
    near = jnp.where(jnp.abs(row_of - base) < 0.5, 1.0 - share, 0.0) + jnp.where(
        jnp.abs(row_of - base - 1.0) < 0.5, share, 0.0
    )
    for p in range(planes):
        blend_rows[p * tall : (p + 1) * tall, :] = (near * planes_ref[p : p + 1, :]).astype(
            jnp.bfloat16
        )
    scale = shift_ref[c]
    spectrum = jnp.concatenate(
        [modes[d] * scale[d : d + 1, :] for d in range(n_cols)], axis=-1
    )
    physical = jnp.dot(
        spectrum, transform_ref[...], precision=HIGHEST, preferred_element_type=jnp.float32
    )
    along = sum(
        jnp.dot(part, blend_ref[...], preferred_element_type=jnp.float32)
        for part in reversed(parts_of(physical))
    )
    for m in range(2):
        picked = jnp.concatenate(
            [along[b * block + m * group : b * block + (m + 1) * group] for b in range(3)], axis=0
        )
        stack = list(parts_of(picked))
        short = depth - 9 * group
        if short:
            stack.append(jnp.zeros((short, picked.shape[1]), jnp.bfloat16))
        stacked = jnp.concatenate(stack, axis=0)
        for t in range(tiles):
            speed = jnp.dot(
                blend_rows[...], stacked[:, t * LANES : (t + 1) * LANES],
                preferred_element_type=jnp.float32,
            )
            speeds[m, t] = speed.reshape(planes, tall, LANES)

    for copy in strip_copies:
        copy.wait_recv()

    lane1 = lax.broadcasted_iota(jnp.int32, (SUB, LANES), 1)
    from_right = {k: lane1 < LANES - k for k in (1, 2)}
    from_left = {k: lane1 >= k for k in (1, 2)}
    halo_lane = lax.broadcasted_iota(jnp.int32, (tall, LANES), 1) < HALO

    def shifted(values, k):
        rolled = [pltpu.roll(v, (LANES - k) % LANES, 1) for v in values]
        if k > 0:
            return [
                jnp.where(from_right[k], rolled[t], rolled[(t + 1) % tiles]) for t in range(tiles)
            ]
        return [jnp.where(from_left[-k], rolled[t], rolled[t - 1]) for t in range(tiles)]

    def rows_of(ref, at, step=0):
        first = SUB + at + step
        return [ref[t, first : first + SUB, :] for t in range(tiles)]

    def tendency(ref, at):
        centre = rows_of(ref, at)
        ups, downs = rows_of(ref, at, 1), rows_of(ref, at, -1)
        ups2, downs2 = rows_of(ref, at, 2), rows_of(ref, at, -2)
        r1, l1, r2, l2 = (shifted(centre, k) for k in (1, -1, 2, -2))
        result = []
        for t in range(tiles):
            w = [coef[n, t, at : at + SUB, :] for n in range(7)]
            rows = w[0] * ups[t] + w[1] * downs[t] + w[5] * (ups2[t] - downs2[t])
            cols = w[2] * r1[t] + w[3] * l1[t] + w[6] * (r2[t] - l2[t])
            result.append((rows + cols) - w[4] * centre[t])
        return result

    def one_plane(p, carry):
        for array, (ref, work, gain) in enumerate(
            ((s_ref, field, None), (k_ref, kappa, 0.25 * TIME_STEP))
        ):
            def put(value):
                return value if gain is None else value * gain

            for t in range(own_tiles):
                at = slice(t * LANES, (t + 1) * LANES)
                work[t, SUB : SUB + HALO, :] = put(above[array, p, :, at])
                work[t, SUB + HALO : SUB + HALO + rows_dev, :] = put(ref[p, :, at])
                work[t, SUB + HALO + rows_dev : SUB + tall, :] = put(below[array, p, :, at])
            from_l = pltpu.roll(strips[0, array], lax.rem(2 * LANES - HALO * (p + 1), LANES), 1)
            from_r = pltpu.roll(strips[1, array], lax.rem(LANES - HALO * p, LANES), 1)
            work[own_tiles, SUB : SUB + tall, :] = put(jnp.where(halo_lane, from_r, from_l))

        for at in range(0, tall, SUB):
            centre = rows_of(kappa, at)
            ups, downs = rows_of(kappa, at, 1), rows_of(kappa, at, -1)
            rights, lefts = shifted(centre, 1), shifted(centre, -1)
            for t in range(tiles):
                u = speeds[0, t, p, at : at + SUB, :]
                v = speeds[1, t, p, at : at + SUB, :]
                u8, v8 = 8.0 * u, 8.0 * v
                east = centre[t] + ups[t] - u8
                west = centre[t] + downs[t] + u8
                north = centre[t] + rights[t] - v8
                south = centre[t] + lefts[t] + v8
                for n, value in enumerate(
                    (east, west, north, south, (east + west) + (north + south), u, v)
                ):
                    coef[n, t, at : at + SUB, :] = value

        for src, dst, span, gain in (
            (field, state_b, (0, tall), 1.0),
            (state_b, state_c, (4, tall - 4), 1.0),
            (state_c, state_d, (4, tall - 4), 2.0),
        ):
            for at in range(*span, SUB):
                slope = tendency(src, at)
                start = rows_of(field, at)
                for t in range(tiles):
                    dst[t, SUB + at : 2 * SUB + at, :] = start[t] + (
                        slope[t] if gain == 1.0 else gain * slope[t]
                    )
        for at in range(HALO, HALO + rows_dev, SUB):
            slope = tendency(state_d, at)
            a, b = rows_of(field, at), rows_of(state_b, at)
            e, g = rows_of(state_c, at), rows_of(state_d, at)
            for t in range(own_tiles):
                sums = (b[t] - a[t]) + 2.0 * e[t] + (g[t] + slope[t])
                o_ref[p, at - HALO : at - HALO + SUB, t * LANES : (t + 1) * LANES] = sums * (
                    1.0 / 3.0
                )
        return carry

    for chunk in range(chunks):
        for copy in row_copies[chunk]:
            copy.wait_recv()
        lax.fori_loop(chunk * per_chunk, (chunk + 1) * per_chunk, one_plane, 0)

    for copy in vel_copies + strip_copies + sum(row_copies, []):
        copy.wait_send()


def solution(mesh):
    n_rows, n_cols = mesh.shape["rows"], mesh.shape["cols"]
    chunks = 4

    def per_device(scalar, diffusivity, vel_modes, offsets):
        planes, rows_dev, cols_dev = scalar.shape
        coarse, coarse_rows, modes_dev = vel_modes.shape
        consts = tables(n_cols, modes_dev, cols_dev, planes, coarse // 2, coarse_rows)
        tiles = cols_dev // LANES + 1
        tall = rows_dev + 2 * HALO
        group = -(-(coarse // 2 * coarse_rows) // 16) * 16
        block = 2 * group + SUB
        depth = consts[4].shape[1]
        partners = 3 * n_cols - 1
        work = pltpu.VMEM((tiles, tall + 2 * SUB, LANES), jnp.float32)
        dma = pltpu.SemaphoreType.DMA
        return pl.pallas_call(
            functools.partial(kernel, n_rows, n_cols, chunks),
            out_shape=jax.ShapeDtypeStruct(scalar.shape, jnp.float32),
            in_specs=[pl.BlockSpec(memory_space=pltpu.VMEM)] * 9,
            out_specs=pl.BlockSpec(memory_space=pltpu.VMEM),
            scratch_shapes=[
                pltpu.VMEM((block, 2 * modes_dev), jnp.float32),
                pltpu.VMEM((n_cols, 3 * block, 2 * modes_dev), jnp.float32),
                pltpu.VMEM((2, 2, rows_dev, LANES), jnp.float32),
                pltpu.VMEM((2, 2, tall, LANES), jnp.float32),
                pltpu.VMEM((2, planes, HALO, cols_dev), jnp.float32),
                pltpu.VMEM((2, planes, HALO, cols_dev), jnp.float32),
                pltpu.VMEM((planes * tall, depth), jnp.bfloat16),
                pltpu.VMEM((2, tiles, planes, tall, LANES), jnp.float32),
                work, work, work, work, work,
                pltpu.VMEM((7, tiles, tall, LANES), jnp.float32),
                dma((partners,)), dma((partners,)),
                dma((6,)), dma((6,)),
                dma((4 * chunks,)), dma((4 * chunks,)),
            ],
            compiler_params=pltpu.CompilerParams(
                collective_id=0, has_side_effects=True, vmem_limit_bytes=40 * 1024 * 1024
            ),
        )(scalar, diffusivity, vel_modes, offsets.reshape(1, rows_dev), *consts)

    return jax.shard_map(
        per_device,
        mesh=mesh,
        in_specs=(
            P(None, "rows", "cols"),
            P(None, "rows", "cols"),
            P(None, "rows", "cols"),
            P("rows"),
        ),
        out_specs=P(None, "rows", "cols"),
        check_vma=False,
    )
```

```python
import functools

import jax
import jax.numpy as jnp
import numpy as np
from jax import lax
from jax.experimental import pallas as pl
from jax.experimental.pallas import tpu as pltpu
from jax.sharding import PartitionSpec as P

TIME_STEP = 0.25
RATIO = 8
HALO = 8
LANES = 128
SUB = 8
MESH = pl.DeviceIdType.MESH
HIGHEST = lax.Precision.HIGHEST


def tables(count, modes_dev, cols_dev, planes, coarse_planes, coarse_rows):
    length = count * modes_dev
    coarse_cols = cols_dev // RATIO
    tiles = cols_dev // LANES + 1
    width = tiles * LANES

    def turn(product):
        return 2.0 * np.pi * (product % length) / length

    wavenum = np.arange(length).reshape(count, modes_dev)
    first = turn(np.arange(count)[:, None, None] * coarse_cols * wavenum[None])
    shift = np.concatenate([np.cos(first) + np.sin(first), np.cos(first) - np.sin(first)], axis=-1)
    shift = shift * (0.5 * TIME_STEP / 12.0)
    places = np.arange(coarse_cols + 3) - 1
    local = turn(wavenum[:, :, None] * places[None, None, :])
    local = np.concatenate([np.cos(local), np.sin(local)], axis=1).reshape(2 * length, -1)
    breadth = -(-local.shape[1] // LANES) * LANES
    transform = np.zeros((2 * length, breadth))
    transform[:, : local.shape[1]] = local
    lane = np.arange(width)
    fine = np.where(lane >= width - HALO, lane - width, np.minimum(lane, cols_dev + HALO - 1))
    col_blend = np.zeros((breadth, width))
    base = fine // RATIO + 1
    share = (fine % RATIO) / RATIO
    col_blend[base, lane] += 1.0 - share
    col_blend[base + 1, lane] += share
    group = -(-coarse_planes * coarse_rows // 16) * 16
    depth = -(-9 * group // LANES) * LANES
    plane_blend = np.zeros((planes, depth))
    row_of = np.full((SUB, depth), -100.0)
    plane = np.arange(planes)
    weights = np.zeros((planes, coarse_planes))
    for p in plane:
        weights[p, p // RATIO % coarse_planes] += 1.0 - (p % RATIO) / RATIO
        weights[p, (p // RATIO + 1) % coarse_planes] += (p % RATIO) / RATIO
    for part in range(3):
        for block in range(3):
            for q in range(coarse_planes):
                for a in range(coarse_rows):
                    at = (part * 3 + block) * group + q * coarse_rows + a
                    plane_blend[:, at] = weights[:, q]
                    row_of[:, at] = block * coarse_rows + a
    as_f32 = functools.partial(np.asarray, dtype=np.float32)
    return (
        as_f32(shift),
        as_f32(transform),
        as_f32(col_blend),
        as_f32(plane_blend),
        as_f32(row_of),
    )


def parts_of(value):
    high = value.astype(jnp.bfloat16)
    rest = value - high.astype(jnp.float32)
    middle = rest.astype(jnp.bfloat16)
    low = (rest - middle.astype(jnp.float32)).astype(jnp.bfloat16)
    return high, middle, low


def kernel(
    n_rows, n_cols, chunks,
    s_hbm, k_hbm, m_hbm, off_hbm, shift_hbm, transform_hbm, blend_hbm, planes_hbm, rowof_hbm,
    o_hbm,
    s_ref, k_ref, m_ref, off_ref, shift_ref, transform_ref, blend_ref, planes_ref, rowof_ref,
    o_ref, load_sem, store_sem,
    message, modes, packed, strips, above, below, blend_rows, speeds,
    field, kappa, state_b, state_c, state_d, coef,
    vel_send, vel_recv, strip_send, strip_recv, row_send, row_recv,
):
    planes, rows_dev, cols_dev = s_ref.shape
    own_tiles = cols_dev // LANES
    tiles = own_tiles + 1
    tall = rows_dev + 2 * HALO
    coarse = m_ref.shape[0]
    coarse_planes = coarse // 2
    coarse_rows = m_ref.shape[1]
    group = modes.shape[1] // 3 // 2 - SUB // 2
    block = 2 * group + SUB
    r = lax.axis_index("rows")
    c = lax.axis_index("cols")
    row_at = {-1: lax.rem(r + n_rows - 1, n_rows), 0: r, 1: lax.rem(r + 1, n_rows)}
    col_at = [c] + [lax.rem(c + d, n_cols) for d in range(1, n_cols)]
    left, right = col_at[n_cols - 1], col_at[1]

    loads = [
        pltpu.make_async_copy(src, dst, load_sem.at[i])
        for i, (src, dst) in enumerate((
            (m_hbm, m_ref), (off_hbm, off_ref), (s_hbm, s_ref), (k_hbm, k_ref),
            (shift_hbm, shift_ref), (transform_hbm, transform_ref), (blend_hbm, blend_ref),
            (planes_hbm, planes_ref), (rowof_hbm, rowof_ref),
        ))
    ]
    barrier = pltpu.get_barrier_semaphore()
    partners = [(dr, d) for d in range(n_cols) for dr in (-1, 0, 1) if (dr, d) != (0, 0)]
    for dr, d in partners:
        pl.semaphore_signal(barrier, inc=1, device_id=(row_at[dr], col_at[d]), device_id_type=MESH)

    for copy in loads:
        copy.start()
    message[...] = jnp.zeros_like(message)
    loads[0].wait()
    loads[1].wait()
    for part in range(coarse):
        at = part // coarse_planes * group + part % coarse_planes * coarse_rows
        once = m_ref[part]
        message[at : at + coarse_rows, :] = jnp.concatenate([once, once], axis=-1)
    message[2 * group :, 0:rows_dev] = jnp.broadcast_to(
        off_ref[...].astype(jnp.float32), (SUB, rows_dev)
    )
    pl.semaphore_wait(barrier, len(partners))

    def send(src, dst, sems, target):
        copy = pltpu.make_async_remote_copy(
            src_ref=src, dst_ref=dst, send_sem=sems[0], recv_sem=sems[1],
            device_id=target, device_id_type=MESH,
        )
        copy.start()
        return copy

    vel_copies = []
    for index, (dr, d) in enumerate(partners):
        vel_copies.append(send(
            message, modes.at[c, pl.ds((1 - dr) * block, block)],
            (vel_send.at[index], vel_recv.at[index]), (row_at[dr], col_at[d]),
        ))

    per_chunk = planes // chunks
    row_copies = []
    for chunk in range(chunks):
        mine = pl.ds(chunk * per_chunk, per_chunk)
        held = []
        for array, ref in enumerate((s_hbm, k_hbm)):
            at = (chunk * 2 + array) * 2
            held.append(send(
                ref.at[mine, pl.ds(0, HALO)], below.at[array, mine],
                (row_send.at[at], row_recv.at[at]), (row_at[-1], c),
            ))
            held.append(send(
                ref.at[mine, pl.ds(rows_dev - HALO, HALO)], above.at[array, mine],
                (row_send.at[at + 1], row_recv.at[at + 1]), (row_at[1], c),
            ))
        row_copies.append(held)

    loads[2].wait()
    loads[3].wait()
    lane8 = lax.broadcasted_iota(jnp.int32, (rows_dev, LANES), 1)
    for side in range(2):
        for array, ref in enumerate((s_ref, k_ref)):
            total = jnp.zeros((rows_dev, LANES), jnp.float32)
            for p in range(planes):
                if side == 0:
                    edge = pltpu.roll(ref[p, :, 0:LANES], (HALO * p) % LANES, 1)
                else:
                    edge = pltpu.roll(ref[p, :, cols_dev - LANES :], (HALO * (p + 1)) % LANES, 1)
                total = jnp.where(lane8 // HALO == p, edge, total)
            packed[side, array] = total
    strip_copies = []
    for side, target in ((0, left), (1, right)):
        there = strips.at[1 - side]
        for index, (dr, first, extent, place) in enumerate((
            (0, 0, rows_dev, HALO),
            (-1, 0, HALO, HALO + rows_dev),
            (1, rows_dev - HALO, HALO, 0),
        )):
            at = side * 3 + index
            strip_copies.append(send(
                packed.at[side, :, pl.ds(first, extent)], there.at[:, pl.ds(place, extent)],
                (strip_send.at[at], strip_recv.at[at]), (row_at[dr], target),
            ))

    modes[c, pl.ds(block, block)] = message[...]
    for copy in loads[4:]:
        copy.wait()
    for copy in vel_copies:
        copy.wait_recv()
    depth = rowof_ref.shape[1]
    offsets_at = jnp.zeros((tall, LANES), jnp.float32)
    lane = lax.broadcasted_iota(jnp.int32, (tall, LANES), 1)
    ext = lax.broadcasted_iota(jnp.int32, (tall, LANES), 0)
    for part in range(3):
        values = modes[c, part * block + 2 * group : (part + 1) * block, :][0:1]
        here = (lane == ext - HALO + rows_dev * (1 - part)) & (lane < rows_dev)
        offsets_at = offsets_at + jnp.where(here, values, 0.0)
    offset = jnp.dot(
        offsets_at, jnp.ones((LANES, depth), jnp.float32), precision=HIGHEST,
        preferred_element_type=jnp.float32,
    )
    fine = lax.broadcasted_iota(jnp.int32, (tall, depth), 0)
    base = (fine // RATIO + (coarse_rows - 1)).astype(jnp.float32) + offset
    share = (fine % RATIO).astype(jnp.float32) / RATIO
    row_of = rowof_ref[0:1, :]
    near = jnp.where(jnp.abs(row_of - base) < 0.5, 1.0 - share, 0.0) + jnp.where(
        jnp.abs(row_of - base - 1.0) < 0.5, share, 0.0
    )
    for p in range(planes):
        blend_rows[p * tall : (p + 1) * tall, :] = (near * planes_ref[p : p + 1, :]).astype(
            jnp.bfloat16
        )
    scale = shift_ref[c]
    spectrum = jnp.concatenate(
        [modes[d] * scale[d : d + 1, :] for d in range(n_cols)], axis=-1
    )
    physical = jnp.dot(
        spectrum, transform_ref[...], precision=HIGHEST, preferred_element_type=jnp.float32
    )
    blend = blend_ref[...].astype(jnp.bfloat16)
    along = sum(
        jnp.dot(part, blend, preferred_element_type=jnp.float32)
        for part in reversed(parts_of(physical))
    )
    for m in range(2):
        picked = jnp.concatenate(
            [along[b * block + m * group : b * block + (m + 1) * group] for b in range(3)], axis=0
        )
        stack = list(parts_of(picked))
        short = depth - 9 * group
        if short:
            stack.append(jnp.zeros((short, picked.shape[1]), jnp.bfloat16))
        stacked = jnp.concatenate(stack, axis=0)
        for t in range(0, tiles, 2):
            wide = min(2, tiles - t)
            speed = jnp.dot(
                blend_rows[...], stacked[:, t * LANES : (t + wide) * LANES],
                preferred_element_type=jnp.float32,
            )
            for n in range(wide):
                speeds[m, t + n] = speed[:, n * LANES : (n + 1) * LANES].reshape(
                    planes, tall, LANES
                )

    for copy in strip_copies:
        copy.wait_recv()

    lane1 = lax.broadcasted_iota(jnp.int32, (SUB, LANES), 1)
    from_right = {k: lane1 < LANES - k for k in (1, 2)}
    from_left = {k: lane1 >= k for k in (1, 2)}
    halo_lane = lax.broadcasted_iota(jnp.int32, (tall, LANES), 1) < HALO

    def shifted(values, k):
        rolled = [pltpu.roll(v, (LANES - k) % LANES, 1) for v in values]
        if k > 0:
            return [
                jnp.where(from_right[k], rolled[t], rolled[(t + 1) % tiles]) for t in range(tiles)
            ]
        return [jnp.where(from_left[-k], rolled[t], rolled[t - 1]) for t in range(tiles)]

    def rows_of(ref, at, step=0):
        first = SUB + at + step
        return [ref[t, first : first + SUB, :] for t in range(tiles)]

    def tendency(ref, at):
        centre = rows_of(ref, at)
        ups, downs = rows_of(ref, at, 1), rows_of(ref, at, -1)
        ups2, downs2 = rows_of(ref, at, 2), rows_of(ref, at, -2)
        r1, l1, r2, l2 = (shifted(centre, k) for k in (1, -1, 2, -2))
        result = []
        for t in range(tiles):
            w = [coef[n, t, at : at + SUB, :] for n in range(7)]
            rows = w[0] * ups[t] + w[1] * downs[t] + w[5] * (ups2[t] - downs2[t])
            cols = w[2] * r1[t] + w[3] * l1[t] + w[6] * (r2[t] - l2[t])
            result.append((rows + cols) - w[4] * centre[t])
        return result

    def one_plane(p, carry):
        for array, (ref, work, gain) in enumerate(
            ((s_ref, field, None), (k_ref, kappa, 0.25 * TIME_STEP))
        ):
            def put(value):
                return value if gain is None else value * gain

            for t in range(own_tiles):
                at = slice(t * LANES, (t + 1) * LANES)
                work[t, SUB : SUB + HALO, :] = put(above[array, p, :, at])
                work[t, SUB + HALO : SUB + HALO + rows_dev, :] = put(ref[p, :, at])
                work[t, SUB + HALO + rows_dev : SUB + tall, :] = put(below[array, p, :, at])
            from_l = pltpu.roll(strips[0, array], lax.rem(2 * LANES - HALO * (p + 1), LANES), 1)
            from_r = pltpu.roll(strips[1, array], lax.rem(LANES - HALO * p, LANES), 1)
            work[own_tiles, SUB : SUB + tall, :] = put(jnp.where(halo_lane, from_r, from_l))

        for at in range(0, tall, SUB):
            centre = rows_of(kappa, at)
            ups, downs = rows_of(kappa, at, 1), rows_of(kappa, at, -1)
            rights, lefts = shifted(centre, 1), shifted(centre, -1)
            for t in range(tiles):
                u = speeds[0, t, p, at : at + SUB, :]
                v = speeds[1, t, p, at : at + SUB, :]
                u8, v8 = 8.0 * u, 8.0 * v
                east = centre[t] + ups[t] - u8
                west = centre[t] + downs[t] + u8
                north = centre[t] + rights[t] - v8
                south = centre[t] + lefts[t] + v8
                for n, value in enumerate(
                    (east, west, north, south, (east + west) + (north + south), u, v)
                ):
                    coef[n, t, at : at + SUB, :] = value

        for src, dst, span, gain in (
            (field, state_b, (0, tall), 1.0),
            (state_b, state_c, (4, tall - 4), 1.0),
            (state_c, state_d, (4, tall - 4), 2.0),
        ):
            for at in range(*span, SUB):
                slope = tendency(src, at)
                start = rows_of(field, at)
                for t in range(tiles):
                    dst[t, SUB + at : 2 * SUB + at, :] = start[t] + (
                        slope[t] if gain == 1.0 else gain * slope[t]
                    )
        for at in range(HALO, HALO + rows_dev, SUB):
            slope = tendency(state_d, at)
            a, b = rows_of(field, at), rows_of(state_b, at)
            e, g = rows_of(state_c, at), rows_of(state_d, at)
            for t in range(own_tiles):
                sums = (b[t] - a[t]) + 2.0 * e[t] + (g[t] + slope[t])
                o_ref[p, at - HALO : at - HALO + SUB, t * LANES : (t + 1) * LANES] = sums * (
                    1.0 / 3.0
                )
        return carry

    stores = []
    for chunk in range(chunks):
        for copy in row_copies[chunk]:
            copy.wait_recv()
        lax.fori_loop(chunk * per_chunk, (chunk + 1) * per_chunk, one_plane, 0)
        done = pl.ds(chunk * per_chunk, per_chunk)
        stores.append(pltpu.make_async_copy(o_ref.at[done], o_hbm.at[done], store_sem.at[chunk]))
        stores[-1].start()

    for copy in stores:
        copy.wait()
    for copy in vel_copies + strip_copies + sum(row_copies, []):
        copy.wait_send()


def solution(mesh):
    n_rows, n_cols = mesh.shape["rows"], mesh.shape["cols"]
    chunks = 4

    def per_device(scalar, diffusivity, vel_modes, offsets):
        planes, rows_dev, cols_dev = scalar.shape
        coarse, coarse_rows, modes_dev = vel_modes.shape
        consts = tables(n_cols, modes_dev, cols_dev, planes, coarse // 2, coarse_rows)
        tiles = cols_dev // LANES + 1
        tall = rows_dev + 2 * HALO
        group = -(-(coarse // 2 * coarse_rows) // 16) * 16
        block = 2 * group + SUB
        depth = consts[4].shape[1]
        partners = 3 * n_cols - 1
        work = pltpu.VMEM((tiles, tall + 2 * SUB, LANES), jnp.float32)
        dma = pltpu.SemaphoreType.DMA
        operands = (scalar, diffusivity, vel_modes, offsets.reshape(1, rows_dev), *consts)
        return pl.pallas_call(
            functools.partial(kernel, n_rows, n_cols, chunks),
            out_shape=jax.ShapeDtypeStruct(scalar.shape, jnp.float32),
            in_specs=[pl.BlockSpec(memory_space=pl.ANY)] * len(operands),
            out_specs=pl.BlockSpec(memory_space=pl.ANY),
            scratch_shapes=[pltpu.VMEM(x.shape, x.dtype) for x in operands] + [
                pltpu.VMEM(scalar.shape, jnp.float32), dma((len(operands),)), dma((chunks,)),
                pltpu.VMEM((block, 2 * modes_dev), jnp.float32),
                pltpu.VMEM((n_cols, 3 * block, 2 * modes_dev), jnp.float32),
                pltpu.VMEM((2, 2, rows_dev, LANES), jnp.float32),
                pltpu.VMEM((2, 2, tall, LANES), jnp.float32),
                pltpu.VMEM((2, planes, HALO, cols_dev), jnp.float32),
                pltpu.VMEM((2, planes, HALO, cols_dev), jnp.float32),
                pltpu.VMEM((planes * tall, depth), jnp.bfloat16),
                pltpu.VMEM((2, tiles, planes, tall, LANES), jnp.float32),
                work, work, work, work, work,
                pltpu.VMEM((7, tiles, tall, LANES), jnp.float32),
                dma((partners,)), dma((partners,)),
                dma((6,)), dma((6,)),
                dma((4 * chunks,)), dma((4 * chunks,)),
            ],
            compiler_params=pltpu.CompilerParams(
                collective_id=0, has_side_effects=True, vmem_limit_bytes=56 * 1024 * 1024
            ),
        )(*operands)

    return jax.shard_map(
        per_device,
        mesh=mesh,
        in_specs=(
            P(None, "rows", "cols"),
            P(None, "rows", "cols"),
            P(None, "rows", "cols"),
            P("rows"),
        ),
        out_specs=P(None, "rows", "cols"),
        check_vma=False,
    )
```

```python
import functools

import jax
import jax.numpy as jnp
import numpy as np
from jax import lax
from jax.experimental import pallas as pl
from jax.experimental.pallas import tpu as pltpu
from jax.sharding import PartitionSpec as P

TIME_STEP = 0.25
RATIO = 8
HALO = 8
LANES = 128
SUB = 8
MESH = pl.DeviceIdType.MESH
HIGHEST = lax.Precision.HIGHEST


def tables(count, modes_dev, cols_dev, planes, coarse_planes, coarse_rows):
    length = count * modes_dev
    coarse_cols = cols_dev // RATIO
    tiles = cols_dev // LANES + 1
    width = tiles * LANES

    def turn(product):
        return 2.0 * np.pi * (product % length) / length

    wavenum = np.arange(length).reshape(count, modes_dev)
    first = turn(np.arange(count)[:, None, None] * coarse_cols * wavenum[None])
    shift = np.concatenate([np.cos(first) + np.sin(first), np.cos(first) - np.sin(first)], axis=-1)
    shift = shift * (0.5 * TIME_STEP / 12.0)
    places = np.arange(coarse_cols + 3) - 1
    local = turn(wavenum[:, :, None] * places[None, None, :])
    local = np.concatenate([np.cos(local), np.sin(local)], axis=1).reshape(2 * length, -1)
    breadth = -(-local.shape[1] // LANES) * LANES
    transform = np.zeros((2 * length, breadth))
    transform[:, : local.shape[1]] = local
    lane = np.arange(width)
    fine = np.where(lane >= width - HALO, lane - width, np.minimum(lane, cols_dev + HALO - 1))
    col_blend = np.zeros((breadth, width))
    base = fine // RATIO + 1
    share = (fine % RATIO) / RATIO
    col_blend[base, lane] += 1.0 - share
    col_blend[base + 1, lane] += share
    group = -(-coarse_planes * coarse_rows // 16) * 16
    depth = -(-9 * group // LANES) * LANES
    plane_blend = np.zeros((planes, depth))
    row_of = np.full((SUB, depth), -100.0)
    plane = np.arange(planes)
    weights = np.zeros((planes, coarse_planes))
    for p in plane:
        weights[p, p // RATIO % coarse_planes] += 1.0 - (p % RATIO) / RATIO
        weights[p, (p // RATIO + 1) % coarse_planes] += (p % RATIO) / RATIO
    for part in range(3):
        for block in range(3):
            for q in range(coarse_planes):
                for a in range(coarse_rows):
                    at = (part * 3 + block) * group + q * coarse_rows + a
                    plane_blend[:, at] = weights[:, q]
                    row_of[:, at] = block * coarse_rows + a
    as_f32 = functools.partial(np.asarray, dtype=np.float32)
    return (
        as_f32(shift),
        as_f32(transform),
        as_f32(col_blend),
        as_f32(plane_blend),
        as_f32(row_of),
    )


def parts_of(value):
    high = value.astype(jnp.bfloat16)
    rest = value - high.astype(jnp.float32)
    middle = rest.astype(jnp.bfloat16)
    low = (rest - middle.astype(jnp.float32)).astype(jnp.bfloat16)
    return high, middle, low


def kernel(
    n_rows, n_cols, chunks,
    s_hbm, k_hbm, m_hbm, off_hbm, shift_hbm, transform_hbm, blend_hbm, planes_hbm, rowof_hbm,
    o_ref,
    s_ref, k_ref, m_ref, off_ref, shift_ref, transform_ref, blend_ref, planes_ref, rowof_ref,
    load_sem,
    message, modes, packed, strips, above, below, blend_rows, speeds,
    field, kappa, state_b, state_c, state_d, coef,
    vel_send, vel_recv, strip_send, strip_recv, row_send, row_recv,
):
    planes, rows_dev, cols_dev = s_ref.shape
    own_tiles = cols_dev // LANES
    tiles = own_tiles + 1
    tall = rows_dev + 2 * HALO
    coarse = m_ref.shape[0]
    coarse_planes = coarse // 2
    coarse_rows = m_ref.shape[1]
    group = modes.shape[1] // 3 // 2 - SUB // 2
    block = 2 * group + SUB
    r = lax.axis_index("rows")
    c = lax.axis_index("cols")
    row_at = {-1: lax.rem(r + n_rows - 1, n_rows), 0: r, 1: lax.rem(r + 1, n_rows)}
    col_at = [c] + [lax.rem(c + d, n_cols) for d in range(1, n_cols)]
    left, right = col_at[n_cols - 1], col_at[1]

    loads = [
        pltpu.make_async_copy(src, dst, load_sem.at[i])
        for i, (src, dst) in enumerate((
            (m_hbm, m_ref), (off_hbm, off_ref), (s_hbm, s_ref), (k_hbm, k_ref),
            (shift_hbm, shift_ref), (transform_hbm, transform_ref), (blend_hbm, blend_ref),
            (planes_hbm, planes_ref), (rowof_hbm, rowof_ref),
        ))
    ]
    barrier = pltpu.get_barrier_semaphore()
    partners = [(dr, d) for d in range(n_cols) for dr in (-1, 0, 1) if (dr, d) != (0, 0)]
    for dr, d in partners:
        pl.semaphore_signal(barrier, inc=1, device_id=(row_at[dr], col_at[d]), device_id_type=MESH)

    for copy in loads:
        copy.start()
    message[...] = jnp.zeros_like(message)
    loads[0].wait()
    loads[1].wait()
    for part in range(coarse):
        at = part // coarse_planes * group + part % coarse_planes * coarse_rows
        once = m_ref[part]
        message[at : at + coarse_rows, :] = jnp.concatenate([once, once], axis=-1)
    message[2 * group :, 0:rows_dev] = jnp.broadcast_to(
        off_ref[...].astype(jnp.float32), (SUB, rows_dev)
    )
    pl.semaphore_wait(barrier, len(partners))

    def send(src, dst, sems, target):
        copy = pltpu.make_async_remote_copy(
            src_ref=src, dst_ref=dst, send_sem=sems[0], recv_sem=sems[1],
            device_id=target, device_id_type=MESH,
        )
        copy.start()
        return copy

    vel_copies = []
    for index, (dr, d) in enumerate(partners):
        vel_copies.append(send(
            message, modes.at[c, pl.ds((1 - dr) * block, block)],
            (vel_send.at[index], vel_recv.at[index]), (row_at[dr], col_at[d]),
        ))

    loads[2].wait()
    loads[3].wait()
    lane8 = lax.broadcasted_iota(jnp.int32, (rows_dev, LANES), 1)
    for side in range(2):
        for array, ref in enumerate((s_ref, k_ref)):
            total = jnp.zeros((rows_dev, LANES), jnp.float32)
            for p in range(planes):
                if side == 0:
                    edge = pltpu.roll(ref[p, :, 0:LANES], (HALO * p) % LANES, 1)
                else:
                    edge = pltpu.roll(ref[p, :, cols_dev - LANES :], (HALO * (p + 1)) % LANES, 1)
                total = jnp.where(lane8 // HALO == p, edge, total)
            packed[side, array] = total
    strip_copies = []
    for side, target in ((0, left), (1, right)):
        there = strips.at[1 - side]
        for index, (dr, first, extent, place) in enumerate((
            (0, 0, rows_dev, HALO),
            (-1, 0, HALO, HALO + rows_dev),
            (1, rows_dev - HALO, HALO, 0),
        )):
            at = side * 3 + index
            strip_copies.append(send(
                packed.at[side, :, pl.ds(first, extent)], there.at[:, pl.ds(place, extent)],
                (strip_send.at[at], strip_recv.at[at]), (row_at[dr], target),
            ))

    per_chunk = planes // chunks
    row_copies = []
    for chunk in range(chunks):
        mine = pl.ds(chunk * per_chunk, per_chunk)
        held = []
        for array, ref in enumerate((s_ref, k_ref)):
            at = (chunk * 2 + array) * 2
            held.append(send(
                ref.at[mine, pl.ds(0, HALO)], below.at[array, mine],
                (row_send.at[at], row_recv.at[at]), (row_at[-1], c),
            ))
            held.append(send(
                ref.at[mine, pl.ds(rows_dev - HALO, HALO)], above.at[array, mine],
                (row_send.at[at + 1], row_recv.at[at + 1]), (row_at[1], c),
            ))
        row_copies.append(held)

    modes[c, pl.ds(block, block)] = message[...]
    for copy in loads[4:]:
        copy.wait()
    for copy in vel_copies:
        copy.wait_recv()
    depth = rowof_ref.shape[1]
    offsets_at = jnp.zeros((tall, LANES), jnp.float32)
    lane = lax.broadcasted_iota(jnp.int32, (tall, LANES), 1)
    ext = lax.broadcasted_iota(jnp.int32, (tall, LANES), 0)
    for part in range(3):
        values = modes[c, part * block + 2 * group : (part + 1) * block, :][0:1]
        here = (lane == ext - HALO + rows_dev * (1 - part)) & (lane < rows_dev)
        offsets_at = offsets_at + jnp.where(here, values, 0.0)
    offset = jnp.dot(
        offsets_at, jnp.ones((LANES, depth), jnp.float32), precision=HIGHEST,
        preferred_element_type=jnp.float32,
    )
    fine = lax.broadcasted_iota(jnp.int32, (tall, depth), 0)
    base = (fine // RATIO + (coarse_rows - 1)).astype(jnp.float32) + offset
    share = (fine % RATIO).astype(jnp.float32) / RATIO
    row_of = rowof_ref[0:1, :]
    near = jnp.where(jnp.abs(row_of - base) < 0.5, 1.0 - share, 0.0) + jnp.where(
        jnp.abs(row_of - base - 1.0) < 0.5, share, 0.0
    )
    for p in range(planes):
        blend_rows[p * tall : (p + 1) * tall, :] = (near * planes_ref[p : p + 1, :]).astype(
            jnp.bfloat16
        )
    scale = shift_ref[c]
    spectrum = jnp.concatenate(
        [modes[d] * scale[d : d + 1, :] for d in range(n_cols)], axis=-1
    )
    physical = jnp.dot(
        spectrum, transform_ref[...], precision=HIGHEST, preferred_element_type=jnp.float32
    )
    blend = blend_ref[...].astype(jnp.bfloat16)
    along = sum(
        jnp.dot(part, blend, preferred_element_type=jnp.float32)
        for part in reversed(parts_of(physical))
    )
    for m in range(2):
        picked = jnp.concatenate(
            [along[b * block + m * group : b * block + (m + 1) * group] for b in range(3)], axis=0
        )
        stack = list(parts_of(picked))
        short = depth - 9 * group
        if short:
            stack.append(jnp.zeros((short, picked.shape[1]), jnp.bfloat16))
        stacked = jnp.concatenate(stack, axis=0)
        for t in range(0, tiles, 2):
            wide = min(2, tiles - t)
            speed = jnp.dot(
                blend_rows[...], stacked[:, t * LANES : (t + wide) * LANES],
                preferred_element_type=jnp.float32,
            )
            for n in range(wide):
                speeds[m, t + n] = speed[:, n * LANES : (n + 1) * LANES].reshape(
                    planes, tall, LANES
                )

    for copy in strip_copies:
        copy.wait_recv()

    lane1 = lax.broadcasted_iota(jnp.int32, (SUB, LANES), 1)
    from_right = {k: lane1 < LANES - k for k in (1, 2)}
    from_left = {k: lane1 >= k for k in (1, 2)}
    halo_lane = lax.broadcasted_iota(jnp.int32, (tall, LANES), 1) < HALO

    def shifted(values, k):
        rolled = [pltpu.roll(v, (LANES - k) % LANES, 1) for v in values]
        if k > 0:
            return [
                jnp.where(from_right[k], rolled[t], rolled[(t + 1) % tiles]) for t in range(tiles)
            ]
        return [jnp.where(from_left[-k], rolled[t], rolled[t - 1]) for t in range(tiles)]

    def rows_of(ref, at, step=0):
        first = SUB + at + step
        return [ref[t, first : first + SUB, :] for t in range(tiles)]

    def tendency(ref, at):
        centre = rows_of(ref, at)
        ups, downs = rows_of(ref, at, 1), rows_of(ref, at, -1)
        ups2, downs2 = rows_of(ref, at, 2), rows_of(ref, at, -2)
        r1, l1, r2, l2 = (shifted(centre, k) for k in (1, -1, 2, -2))
        result = []
        for t in range(tiles):
            w = [coef[n, t, at : at + SUB, :] for n in range(7)]
            rows = w[0] * ups[t] + w[1] * downs[t] + w[5] * (ups2[t] - downs2[t])
            cols = w[2] * r1[t] + w[3] * l1[t] + w[6] * (r2[t] - l2[t])
            result.append((rows + cols) - w[4] * centre[t])
        return result

    def one_plane(p, carry):
        for array, (ref, work, gain) in enumerate(
            ((s_ref, field, None), (k_ref, kappa, 0.25 * TIME_STEP))
        ):
            def put(value):
                return value if gain is None else value * gain

            for t in range(own_tiles):
                at = slice(t * LANES, (t + 1) * LANES)
                work[t, SUB : SUB + HALO, :] = put(above[array, p, :, at])
                work[t, SUB + HALO : SUB + HALO + rows_dev, :] = put(ref[p, :, at])
                work[t, SUB + HALO + rows_dev : SUB + tall, :] = put(below[array, p, :, at])
            from_l = pltpu.roll(strips[0, array], lax.rem(2 * LANES - HALO * (p + 1), LANES), 1)
            from_r = pltpu.roll(strips[1, array], lax.rem(LANES - HALO * p, LANES), 1)
            work[own_tiles, SUB : SUB + tall, :] = put(jnp.where(halo_lane, from_r, from_l))

        for at in range(0, tall, SUB):
            centre = rows_of(kappa, at)
            ups, downs = rows_of(kappa, at, 1), rows_of(kappa, at, -1)
            rights, lefts = shifted(centre, 1), shifted(centre, -1)
            for t in range(tiles):
                u = speeds[0, t, p, at : at + SUB, :]
                v = speeds[1, t, p, at : at + SUB, :]
                u8, v8 = 8.0 * u, 8.0 * v
                east = centre[t] + ups[t] - u8
                west = centre[t] + downs[t] + u8
                north = centre[t] + rights[t] - v8
                south = centre[t] + lefts[t] + v8
                for n, value in enumerate(
                    (east, west, north, south, (east + west) + (north + south), u, v)
                ):
                    coef[n, t, at : at + SUB, :] = value

        for src, dst, span, gain in (
            (field, state_b, (0, tall), 1.0),
            (state_b, state_c, (4, tall - 4), 1.0),
            (state_c, state_d, (4, tall - 4), 2.0),
        ):
            for at in range(*span, SUB):
                slope = tendency(src, at)
                start = rows_of(field, at)
                for t in range(tiles):
                    dst[t, SUB + at : 2 * SUB + at, :] = start[t] + (
                        slope[t] if gain == 1.0 else gain * slope[t]
                    )
        for at in range(HALO, HALO + rows_dev, SUB):
            slope = tendency(state_d, at)
            a, b = rows_of(field, at), rows_of(state_b, at)
            e, g = rows_of(state_c, at), rows_of(state_d, at)
            for t in range(own_tiles):
                sums = (b[t] - a[t]) + 2.0 * e[t] + (g[t] + slope[t])
                o_ref[p, at - HALO : at - HALO + SUB, t * LANES : (t + 1) * LANES] = sums * (
                    1.0 / 3.0
                )
        return carry

    for chunk in range(chunks):
        for copy in row_copies[chunk]:
            copy.wait_recv()
        lax.fori_loop(chunk * per_chunk, (chunk + 1) * per_chunk, one_plane, 0)

    for copy in vel_copies + strip_copies + sum(row_copies, []):
        copy.wait_send()


def solution(mesh):
    n_rows, n_cols = mesh.shape["rows"], mesh.shape["cols"]
    chunks = 4

    def per_device(scalar, diffusivity, vel_modes, offsets):
        planes, rows_dev, cols_dev = scalar.shape
        coarse, coarse_rows, modes_dev = vel_modes.shape
        consts = tables(n_cols, modes_dev, cols_dev, planes, coarse // 2, coarse_rows)
        tiles = cols_dev // LANES + 1
        tall = rows_dev + 2 * HALO
        group = -(-(coarse // 2 * coarse_rows) // 16) * 16
        block = 2 * group + SUB
        depth = consts[4].shape[1]
        partners = 3 * n_cols - 1
        work = pltpu.VMEM((tiles, tall + 2 * SUB, LANES), jnp.float32)
        dma = pltpu.SemaphoreType.DMA
        operands = (scalar, diffusivity, vel_modes, offsets.reshape(1, rows_dev), *consts)
        return pl.pallas_call(
            functools.partial(kernel, n_rows, n_cols, chunks),
            out_shape=jax.ShapeDtypeStruct(scalar.shape, jnp.float32),
            in_specs=[pl.BlockSpec(memory_space=pl.ANY)] * len(operands),
            out_specs=pl.BlockSpec(memory_space=pltpu.VMEM),
            scratch_shapes=[pltpu.VMEM(x.shape, x.dtype) for x in operands] + [
                dma((len(operands),)),
                pltpu.VMEM((block, 2 * modes_dev), jnp.float32),
                pltpu.VMEM((n_cols, 3 * block, 2 * modes_dev), jnp.float32),
                pltpu.VMEM((2, 2, rows_dev, LANES), jnp.float32),
                pltpu.VMEM((2, 2, tall, LANES), jnp.float32),
                pltpu.VMEM((2, planes, HALO, cols_dev), jnp.float32),
                pltpu.VMEM((2, planes, HALO, cols_dev), jnp.float32),
                pltpu.VMEM((planes * tall, depth), jnp.bfloat16),
                pltpu.VMEM((2, tiles, planes, tall, LANES), jnp.float32),
                work, work, work, work, work,
                pltpu.VMEM((7, tiles, tall, LANES), jnp.float32),
                dma((partners,)), dma((partners,)),
                dma((6,)), dma((6,)),
                dma((4 * chunks,)), dma((4 * chunks,)),
            ],
            compiler_params=pltpu.CompilerParams(
                collective_id=0, has_side_effects=True, vmem_limit_bytes=56 * 1024 * 1024
            ),
        )(*operands)

    return jax.shard_map(
        per_device,
        mesh=mesh,
        in_specs=(
            P(None, "rows", "cols"),
            P(None, "rows", "cols"),
            P(None, "rows", "cols"),
            P("rows"),
        ),
        out_specs=P(None, "rows", "cols"),
        check_vma=False,
    )
```

```python
import functools

import jax
import jax.numpy as jnp
import numpy as np
from jax import lax
from jax.experimental import pallas as pl
from jax.experimental.pallas import tpu as pltpu
from jax.sharding import PartitionSpec as P

TIME_STEP = 0.25
RATIO = 8
HALO = 8
LANES = 128
SUB = 8
MESH = pl.DeviceIdType.MESH
HIGHEST = lax.Precision.HIGHEST


def tables(count, modes_dev, cols_dev, planes, coarse_planes, coarse_rows):
    length = count * modes_dev
    coarse_cols = cols_dev // RATIO
    tiles = cols_dev // LANES + 1
    width = tiles * LANES

    def turn(product):
        return 2.0 * np.pi * (product % length) / length

    wavenum = np.arange(length).reshape(count, modes_dev)
    first = turn(np.arange(count)[:, None, None] * coarse_cols * wavenum[None])
    shift = np.concatenate([np.cos(first) + np.sin(first), np.cos(first) - np.sin(first)], axis=-1)
    shift = shift * (0.5 * TIME_STEP / 12.0)
    places = np.arange(coarse_cols + 3) - 1
    local = turn(wavenum[:, :, None] * places[None, None, :])
    local = np.concatenate([np.cos(local), np.sin(local)], axis=1).reshape(2 * length, -1)
    breadth = -(-local.shape[1] // LANES) * LANES
    transform = np.zeros((2 * length, breadth))
    transform[:, : local.shape[1]] = local
    lane = np.arange(width)
    fine = np.where(lane >= width - HALO, lane - width, np.minimum(lane, cols_dev + HALO - 1))
    col_blend = np.zeros((breadth, width))
    base = fine // RATIO + 1
    share = (fine % RATIO) / RATIO
    col_blend[base, lane] += 1.0 - share
    col_blend[base + 1, lane] += share
    group = -(-coarse_planes * coarse_rows // 16) * 16
    depth = -(-9 * group // LANES) * LANES
    plane_blend = np.zeros((planes, depth))
    row_of = np.full((SUB, depth), -100.0)
    plane = np.arange(planes)
    weights = np.zeros((planes, coarse_planes))
    for p in plane:
        weights[p, p // RATIO % coarse_planes] += 1.0 - (p % RATIO) / RATIO
        weights[p, (p // RATIO + 1) % coarse_planes] += (p % RATIO) / RATIO
    for part in range(3):
        for block in range(3):
            for q in range(coarse_planes):
                for a in range(coarse_rows):
                    at = (part * 3 + block) * group + q * coarse_rows + a
                    plane_blend[:, at] = weights[:, q]
                    row_of[:, at] = block * coarse_rows + a
    as_f32 = functools.partial(np.asarray, dtype=np.float32)
    return (
        as_f32(shift),
        as_f32(transform),
        as_f32(col_blend),
        as_f32(plane_blend),
        as_f32(row_of),
    )


def parts_of(value):
    high = value.astype(jnp.bfloat16)
    rest = value - high.astype(jnp.float32)
    middle = rest.astype(jnp.bfloat16)
    low = (rest - middle.astype(jnp.float32)).astype(jnp.bfloat16)
    return high, middle, low


def kernel(
    n_rows, n_cols, chunks,
    s_hbm, k_hbm, m_hbm, off_hbm, shift_hbm, transform_hbm, blend_hbm, planes_hbm, rowof_hbm,
    o_ref,
    s_ref, k_ref, m_ref, off_ref, shift_ref, transform_ref, blend_ref, planes_ref, rowof_ref,
    load_sem,
    message, modes, packed, strips, above, below, blend_rows, speeds,
    field, kappa, state_b, state_c, state_d, coef,
    vel_send, vel_recv, strip_send, strip_recv, row_send, row_recv,
):
    planes, rows_dev, cols_dev = s_ref.shape
    own_tiles = cols_dev // LANES
    tiles = own_tiles + 1
    tall = rows_dev + 2 * HALO
    coarse = m_ref.shape[0]
    coarse_planes = coarse // 2
    coarse_rows = m_ref.shape[1]
    group = modes.shape[1] // 3 // 2 - SUB // 2
    block = 2 * group + SUB
    r = lax.axis_index("rows")
    c = lax.axis_index("cols")
    row_at = {-1: lax.rem(r + n_rows - 1, n_rows), 0: r, 1: lax.rem(r + 1, n_rows)}
    col_at = [c] + [lax.rem(c + d, n_cols) for d in range(1, n_cols)]
    left, right = col_at[n_cols - 1], col_at[1]

    loads = [
        pltpu.make_async_copy(src, dst, load_sem.at[i])
        for i, (src, dst) in enumerate((
            (m_hbm, m_ref), (off_hbm, off_ref), (s_hbm, s_ref), (k_hbm, k_ref),
            (shift_hbm, shift_ref), (transform_hbm, transform_ref), (blend_hbm, blend_ref),
            (planes_hbm, planes_ref), (rowof_hbm, rowof_ref),
        ))
    ]
    barrier = pltpu.get_barrier_semaphore()
    partners = [(dr, d) for d in range(n_cols) for dr in (-1, 0, 1) if (dr, d) != (0, 0)]
    for dr, d in partners:
        pl.semaphore_signal(barrier, inc=1, device_id=(row_at[dr], col_at[d]), device_id_type=MESH)

    for copy in loads:
        copy.start()
    message[...] = jnp.zeros_like(message)
    loads[0].wait()
    loads[1].wait()
    for part in range(coarse):
        at = part // coarse_planes * group + part % coarse_planes * coarse_rows
        once = m_ref[part]
        message[at : at + coarse_rows, :] = jnp.concatenate([once, once], axis=-1)
    message[2 * group :, 0:rows_dev] = jnp.broadcast_to(
        off_ref[...].astype(jnp.float32), (SUB, rows_dev)
    )
    pl.semaphore_wait(barrier, len(partners))

    def send(src, dst, sems, target):
        copy = pltpu.make_async_remote_copy(
            src_ref=src, dst_ref=dst, send_sem=sems[0], recv_sem=sems[1],
            device_id=target, device_id_type=MESH,
        )
        copy.start()
        return copy

    vel_copies = []
    for index, (dr, d) in enumerate(partners):
        vel_copies.append(send(
            message, modes.at[c, pl.ds((1 - dr) * block, block)],
            (vel_send.at[index], vel_recv.at[index]), (row_at[dr], col_at[d]),
        ))

    loads[2].wait()
    loads[3].wait()
    lane8 = lax.broadcasted_iota(jnp.int32, (rows_dev, LANES), 1)
    for side in range(2):
        for array, ref in enumerate((s_ref, k_ref)):
            total = jnp.zeros((rows_dev, LANES), jnp.float32)
            for p in range(planes):
                if side == 0:
                    edge = pltpu.roll(ref[p, :, 0:LANES], (HALO * p) % LANES, 1)
                else:
                    edge = pltpu.roll(ref[p, :, cols_dev - LANES :], (HALO * (p + 1)) % LANES, 1)
                total = jnp.where(lane8 // HALO == p, edge, total)
            packed[side, array] = total
    strip_copies = []
    for side, target in ((0, left), (1, right)):
        there = strips.at[1 - side]
        for index, (dr, first, extent, place) in enumerate((
            (0, 0, rows_dev, HALO),
            (-1, 0, HALO, HALO + rows_dev),
            (1, rows_dev - HALO, HALO, 0),
        )):
            at = side * 3 + index
            strip_copies.append(send(
                packed.at[side, :, pl.ds(first, extent)], there.at[:, pl.ds(place, extent)],
                (strip_send.at[at], strip_recv.at[at]), (row_at[dr], target),
            ))

    per_chunk = planes // chunks

    def row_copies(chunk):
        mine = pl.ds(chunk * per_chunk, per_chunk)
        held = []
        for array, ref in enumerate((s_ref, k_ref)):
            at = (chunk * 2 + array) * 2
            for side, (dr, first, there) in enumerate((
                (-1, 0, below), (1, rows_dev - HALO, above),
            )):
                held.append(pltpu.make_async_remote_copy(
                    src_ref=ref.at[mine, pl.ds(first, HALO)], dst_ref=there.at[array, mine],
                    send_sem=row_send.at[at + side], recv_sem=row_recv.at[at + side],
                    device_id=(row_at[dr], c), device_id_type=MESH,
                ))
        return held

    def start_rows(chunk, carry):
        for copy in row_copies(chunk):
            copy.start()
        return carry

    lax.fori_loop(0, chunks, start_rows, 0)

    modes[c, pl.ds(block, block)] = message[...]
    for copy in loads[4:]:
        copy.wait()
    for copy in vel_copies:
        copy.wait_recv()
    depth = rowof_ref.shape[1]
    offsets_at = jnp.zeros((tall, LANES), jnp.float32)
    lane = lax.broadcasted_iota(jnp.int32, (tall, LANES), 1)
    ext = lax.broadcasted_iota(jnp.int32, (tall, LANES), 0)
    for part in range(3):
        values = modes[c, part * block + 2 * group : (part + 1) * block, :][0:1]
        here = (lane == ext - HALO + rows_dev * (1 - part)) & (lane < rows_dev)
        offsets_at = offsets_at + jnp.where(here, values, 0.0)
    offset = jnp.dot(
        offsets_at, jnp.ones((LANES, depth), jnp.float32), preferred_element_type=jnp.float32
    )
    fine = lax.broadcasted_iota(jnp.int32, (tall, depth), 0)
    base = (fine // RATIO + (coarse_rows - 1)).astype(jnp.float32) + offset
    share = (fine % RATIO).astype(jnp.float32) / RATIO
    row_of = rowof_ref[0:1, :]
    near = jnp.where(jnp.abs(row_of - base) < 0.5, 1.0 - share, 0.0) + jnp.where(
        jnp.abs(row_of - base - 1.0) < 0.5, share, 0.0
    )
    for p in range(planes):
        blend_rows[p * tall : (p + 1) * tall, :] = (near * planes_ref[p : p + 1, :]).astype(
            jnp.bfloat16
        )
    scale = shift_ref[c]
    spectrum = jnp.concatenate(
        [modes[d] * scale[d : d + 1, :] for d in range(n_cols)], axis=-1
    )
    physical = jnp.dot(
        spectrum, transform_ref[...], precision=HIGHEST, preferred_element_type=jnp.float32
    )
    blend = blend_ref[...].astype(jnp.bfloat16)
    along = sum(
        jnp.dot(part, blend, preferred_element_type=jnp.float32)
        for part in reversed(parts_of(physical))
    )
    for m in range(2):
        picked = jnp.concatenate(
            [along[b * block + m * group : b * block + (m + 1) * group] for b in range(3)], axis=0
        )
        stack = list(parts_of(picked))
        short = depth - 9 * group
        if short:
            stack.append(jnp.zeros((short, picked.shape[1]), jnp.bfloat16))
        stacked = jnp.concatenate(stack, axis=0)
        for t in range(0, tiles, 2):
            wide = min(2, tiles - t)
            speed = jnp.dot(
                blend_rows[...], stacked[:, t * LANES : (t + wide) * LANES],
                preferred_element_type=jnp.float32,
            )
            for n in range(wide):
                speeds[m, t + n] = speed[:, n * LANES : (n + 1) * LANES].reshape(
                    planes, tall, LANES
                )

    for copy in strip_copies:
        copy.wait_recv()

    lane1 = lax.broadcasted_iota(jnp.int32, (SUB, LANES), 1)
    from_right = {k: lane1 < LANES - k for k in (1, 2)}
    from_left = {k: lane1 >= k for k in (1, 2)}
    halo_lane = lax.broadcasted_iota(jnp.int32, (tall, LANES), 1) < HALO

    def shifted(values, k):
        rolled = [pltpu.roll(v, (LANES - k) % LANES, 1) for v in values]
        if k > 0:
            return [
                jnp.where(from_right[k], rolled[t], rolled[(t + 1) % tiles]) for t in range(tiles)
            ]
        return [jnp.where(from_left[-k], rolled[t], rolled[t - 1]) for t in range(tiles)]

    def rows_of(ref, at, step=0):
        first = SUB + at + step
        return [ref[t, first : first + SUB, :] for t in range(tiles)]

    def tendency(ref, at):
        centre = rows_of(ref, at)
        ups, downs = rows_of(ref, at, 1), rows_of(ref, at, -1)
        ups2, downs2 = rows_of(ref, at, 2), rows_of(ref, at, -2)
        r1, l1, r2, l2 = (shifted(centre, k) for k in (1, -1, 2, -2))
        result = []
        for t in range(tiles):
            w = [coef[n, t, at : at + SUB, :] for n in range(7)]
            rows = w[0] * ups[t] + w[1] * downs[t] + w[5] * (ups2[t] - downs2[t])
            cols = w[2] * r1[t] + w[3] * l1[t] + w[6] * (r2[t] - l2[t])
            result.append((rows + cols) - w[4] * centre[t])
        return result

    def one_plane(p, carry):
        for array, (ref, work, gain) in enumerate(
            ((s_ref, field, None), (k_ref, kappa, 0.25 * TIME_STEP))
        ):
            def put(value):
                return value if gain is None else value * gain

            for t in range(own_tiles):
                at = slice(t * LANES, (t + 1) * LANES)
                work[t, SUB : SUB + HALO, :] = put(above[array, p, :, at])
                work[t, SUB + HALO : SUB + HALO + rows_dev, :] = put(ref[p, :, at])
                work[t, SUB + HALO + rows_dev : SUB + tall, :] = put(below[array, p, :, at])
            from_l = pltpu.roll(strips[0, array], lax.rem(2 * LANES - HALO * (p + 1), LANES), 1)
            from_r = pltpu.roll(strips[1, array], lax.rem(LANES - HALO * p, LANES), 1)
            work[own_tiles, SUB : SUB + tall, :] = put(jnp.where(halo_lane, from_r, from_l))

        for at in range(0, tall, SUB):
            centre = rows_of(kappa, at)
            ups, downs = rows_of(kappa, at, 1), rows_of(kappa, at, -1)
            rights, lefts = shifted(centre, 1), shifted(centre, -1)
            for t in range(tiles):
                u = speeds[0, t, p, at : at + SUB, :]
                v = speeds[1, t, p, at : at + SUB, :]
                u8, v8 = 8.0 * u, 8.0 * v
                east = centre[t] + ups[t] - u8
                west = centre[t] + downs[t] + u8
                north = centre[t] + rights[t] - v8
                south = centre[t] + lefts[t] + v8
                for n, value in enumerate(
                    (east, west, north, south, (east + west) + (north + south), u, v)
                ):
                    coef[n, t, at : at + SUB, :] = value

        for src, dst, span, gain in (
            (field, state_b, (0, tall), 1.0),
            (state_b, state_c, (4, tall - 4), 1.0),
            (state_c, state_d, (4, tall - 4), 2.0),
        ):
            for at in range(*span, SUB):
                slope = tendency(src, at)
                start = rows_of(field, at)
                for t in range(tiles):
                    dst[t, SUB + at : 2 * SUB + at, :] = start[t] + (
                        slope[t] if gain == 1.0 else gain * slope[t]
                    )
        for at in range(HALO, HALO + rows_dev, SUB):
            slope = tendency(state_d, at)
            a, b = rows_of(field, at), rows_of(state_b, at)
            e, g = rows_of(state_c, at), rows_of(state_d, at)
            for t in range(own_tiles):
                sums = (b[t] - a[t]) + 2.0 * e[t] + (g[t] + slope[t])
                o_ref[p, at - HALO : at - HALO + SUB, t * LANES : (t + 1) * LANES] = sums * (
                    1.0 / 3.0
                )
        return carry

    def one_chunk(chunk, carry):
        for copy in row_copies(chunk):
            copy.wait_recv()
        return lax.fori_loop(chunk * per_chunk, (chunk + 1) * per_chunk, one_plane, carry)

    lax.fori_loop(0, chunks, one_chunk, 0)

    def end_rows(chunk, carry):
        for copy in row_copies(chunk):
            copy.wait_send()
        return carry

    lax.fori_loop(0, chunks, end_rows, 0)
    for copy in vel_copies + strip_copies:
        copy.wait_send()


def solution(mesh):
    n_rows, n_cols = mesh.shape["rows"], mesh.shape["cols"]
    chunks = 8

    def per_device(scalar, diffusivity, vel_modes, offsets):
        planes, rows_dev, cols_dev = scalar.shape
        coarse, coarse_rows, modes_dev = vel_modes.shape
        consts = tables(n_cols, modes_dev, cols_dev, planes, coarse // 2, coarse_rows)
        tiles = cols_dev // LANES + 1
        tall = rows_dev + 2 * HALO
        group = -(-(coarse // 2 * coarse_rows) // 16) * 16
        block = 2 * group + SUB
        depth = consts[4].shape[1]
        partners = 3 * n_cols - 1
        work = pltpu.VMEM((tiles, tall + 2 * SUB, LANES), jnp.float32)
        dma = pltpu.SemaphoreType.DMA
        operands = (scalar, diffusivity, vel_modes, offsets.reshape(1, rows_dev), *consts)
        return pl.pallas_call(
            functools.partial(kernel, n_rows, n_cols, chunks),
            out_shape=jax.ShapeDtypeStruct(scalar.shape, jnp.float32),
            in_specs=[pl.BlockSpec(memory_space=pl.ANY)] * len(operands),
            out_specs=pl.BlockSpec(memory_space=pltpu.VMEM),
            scratch_shapes=[pltpu.VMEM(x.shape, x.dtype) for x in operands] + [
                dma((len(operands),)),
                pltpu.VMEM((block, 2 * modes_dev), jnp.float32),
                pltpu.VMEM((n_cols, 3 * block, 2 * modes_dev), jnp.float32),
                pltpu.VMEM((2, 2, rows_dev, LANES), jnp.float32),
                pltpu.VMEM((2, 2, tall, LANES), jnp.float32),
                pltpu.VMEM((2, planes, HALO, cols_dev), jnp.float32),
                pltpu.VMEM((2, planes, HALO, cols_dev), jnp.float32),
                pltpu.VMEM((planes * tall, depth), jnp.bfloat16),
                pltpu.VMEM((2, tiles, planes, tall, LANES), jnp.float32),
                work, work, work, work, work,
                pltpu.VMEM((7, tiles, tall, LANES), jnp.float32),
                dma((partners,)), dma((partners,)),
                dma((6,)), dma((6,)),
                dma((4 * chunks,)), dma((4 * chunks,)),
            ],
            compiler_params=pltpu.CompilerParams(
                collective_id=0, has_side_effects=True, vmem_limit_bytes=40 * 1024 * 1024
            ),
        )(*operands)

    return jax.shard_map(
        per_device,
        mesh=mesh,
        in_specs=(
            P(None, "rows", "cols"),
            P(None, "rows", "cols"),
            P(None, "rows", "cols"),
            P("rows"),
        ),
        out_specs=P(None, "rows", "cols"),
        check_vma=False,
    )
```

```python
import functools

import jax
import jax.numpy as jnp
import numpy as np
from jax import lax
from jax.experimental import pallas as pl
from jax.experimental.pallas import tpu as pltpu
from jax.sharding import PartitionSpec as P

TIME_STEP = 0.25
RATIO = 8
HALO = 8
LANES = 128
SUB = 8
MESH = pl.DeviceIdType.MESH
HIGHEST = lax.Precision.HIGHEST


def tables(count, modes_dev, cols_dev, planes, coarse_planes, coarse_rows):
    length = count * modes_dev
    coarse_cols = cols_dev // RATIO
    tiles = cols_dev // LANES + 1
    width = tiles * LANES

    def turn(product):
        return 2.0 * np.pi * (product % length) / length

    wavenum = np.arange(length).reshape(count, modes_dev)
    first = turn(np.arange(count)[:, None, None] * coarse_cols * wavenum[None])
    shift = np.concatenate([np.cos(first) + np.sin(first), np.cos(first) - np.sin(first)], axis=-1)
    shift = shift * (0.5 * TIME_STEP / 12.0)
    places = np.arange(coarse_cols + 3) - 1
    local = turn(wavenum[:, :, None] * places[None, None, :])
    local = np.concatenate([np.cos(local), np.sin(local)], axis=1).reshape(2 * length, -1)
    breadth = -(-local.shape[1] // LANES) * LANES
    transform = np.zeros((2 * length, breadth))
    transform[:, : local.shape[1]] = local
    lane = np.arange(width)
    fine = np.where(lane >= width - HALO, lane - width, np.minimum(lane, cols_dev + HALO - 1))
    col_blend = np.zeros((breadth, width))
    base = fine // RATIO + 1
    share = (fine % RATIO) / RATIO
    col_blend[base, lane] += 1.0 - share
    col_blend[base + 1, lane] += share
    group = -(-coarse_planes * coarse_rows // 16) * 16
    depth = -(-9 * group // LANES) * LANES
    plane_blend = np.zeros((planes, depth))
    row_of = np.full((SUB, depth), -100.0)
    plane = np.arange(planes)
    weights = np.zeros((planes, coarse_planes))
    for p in plane:
        weights[p, p // RATIO % coarse_planes] += 1.0 - (p % RATIO) / RATIO
        weights[p, (p // RATIO + 1) % coarse_planes] += (p % RATIO) / RATIO
    for part in range(3):
        for block in range(3):
            for q in range(coarse_planes):
                for a in range(coarse_rows):
                    at = (part * 3 + block) * group + q * coarse_rows + a
                    plane_blend[:, at] = weights[:, q]
                    row_of[:, at] = block * coarse_rows + a
    as_f32 = functools.partial(np.asarray, dtype=np.float32)
    return (
        as_f32(shift),
        as_f32(transform),
        as_f32(col_blend),
        as_f32(plane_blend),
        as_f32(row_of),
    )


def parts_of(value):
    high = value.astype(jnp.bfloat16)
    rest = value - high.astype(jnp.float32)
    middle = rest.astype(jnp.bfloat16)
    low = (rest - middle.astype(jnp.float32)).astype(jnp.bfloat16)
    return high, middle, low


def kernel(
    n_rows, n_cols, chunks,
    s_hbm, k_hbm, m_hbm, off_hbm, shift_hbm, transform_hbm, blend_hbm, planes_hbm, rowof_hbm,
    o_ref,
    s_ref, k_ref, m_ref, off_ref, shift_ref, transform_ref, blend_ref, planes_ref, rowof_ref,
    load_sem,
    message, modes, packed, strips, above, below, blend_rows, speeds,
    field, kappa, state_b, state_c, state_d, coef,
    vel_send, vel_recv, strip_send, strip_recv, row_send, row_recv,
):
    planes, rows_dev, cols_dev = s_ref.shape
    own_tiles = cols_dev // LANES
    tiles = own_tiles + 1
    tall = rows_dev + 2 * HALO
    coarse = m_ref.shape[0]
    coarse_planes = coarse // 2
    coarse_rows = m_ref.shape[1]
    group = modes.shape[1] // 3 // 2 - SUB // 2
    block = 2 * group + SUB
    r = lax.axis_index("rows")
    c = lax.axis_index("cols")
    row_at = {-1: lax.rem(r + n_rows - 1, n_rows), 0: r, 1: lax.rem(r + 1, n_rows)}
    col_at = [c] + [lax.rem(c + d, n_cols) for d in range(1, n_cols)]
    left, right = col_at[n_cols - 1], col_at[1]

    loads = [
        pltpu.make_async_copy(src, dst, load_sem.at[i])
        for i, (src, dst) in enumerate((
            (m_hbm, m_ref), (off_hbm, off_ref), (s_hbm, s_ref), (k_hbm, k_ref),
            (shift_hbm, shift_ref), (transform_hbm, transform_ref), (blend_hbm, blend_ref),
            (planes_hbm, planes_ref), (rowof_hbm, rowof_ref),
        ))
    ]
    barrier = pltpu.get_barrier_semaphore()
    partners = [(dr, d) for d in range(n_cols) for dr in (-1, 0, 1) if (dr, d) != (0, 0)]
    for dr, d in partners:
        pl.semaphore_signal(barrier, inc=1, device_id=(row_at[dr], col_at[d]), device_id_type=MESH)

    for copy in loads:
        copy.start()
    message[...] = jnp.zeros_like(message)
    loads[0].wait()
    loads[1].wait()
    for part in range(coarse):
        at = part // coarse_planes * group + part % coarse_planes * coarse_rows
        once = m_ref[part]
        message[at : at + coarse_rows, :] = jnp.concatenate([once, once], axis=-1)
    message[2 * group :, 0:rows_dev] = jnp.broadcast_to(
        off_ref[...].astype(jnp.float32), (SUB, rows_dev)
    )
    pl.semaphore_wait(barrier, len(partners))

    def send(src, dst, sems, target):
        copy = pltpu.make_async_remote_copy(
            src_ref=src, dst_ref=dst, send_sem=sems[0], recv_sem=sems[1],
            device_id=target, device_id_type=MESH,
        )
        copy.start()
        return copy

    vel_copies = []
    for index, (dr, d) in enumerate(partners):
        vel_copies.append(send(
            message, modes.at[c, pl.ds((1 - dr) * block, block)],
            (vel_send.at[index], vel_recv.at[index]), (row_at[dr], col_at[d]),
        ))

    loads[2].wait()
    loads[3].wait()
    lane8 = lax.broadcasted_iota(jnp.int32, (rows_dev, LANES), 1)
    for side in range(2):
        for array, ref in enumerate((s_ref, k_ref)):
            total = jnp.zeros((rows_dev, LANES), jnp.float32)
            for p in range(planes):
                if side == 0:
                    edge = pltpu.roll(ref[p, :, 0:LANES], (HALO * p) % LANES, 1)
                else:
                    edge = pltpu.roll(ref[p, :, cols_dev - LANES :], (HALO * (p + 1)) % LANES, 1)
                total = jnp.where(lane8 // HALO == p, edge, total)
            packed[side, array] = total
    strip_copies = []
    for side, target in ((0, left), (1, right)):
        there = strips.at[1 - side]
        for index, (dr, first, extent, place) in enumerate((
            (0, 0, rows_dev, HALO),
            (-1, 0, HALO, HALO + rows_dev),
            (1, rows_dev - HALO, HALO, 0),
        )):
            at = side * 3 + index
            strip_copies.append(send(
                packed.at[side, :, pl.ds(first, extent)], there.at[:, pl.ds(place, extent)],
                (strip_send.at[at], strip_recv.at[at]), (row_at[dr], target),
            ))

    per_chunk = planes // chunks

    def row_copies(chunk):
        mine = pl.ds(chunk * per_chunk, per_chunk)
        held = []
        for array, ref in enumerate((s_ref, k_ref)):
            at = (chunk * 2 + array) * 2
            for side, (dr, first, there) in enumerate((
                (-1, 0, below), (1, rows_dev - HALO, above),
            )):
                held.append(pltpu.make_async_remote_copy(
                    src_ref=ref.at[mine, pl.ds(first, HALO)], dst_ref=there.at[array, mine],
                    send_sem=row_send.at[at + side], recv_sem=row_recv.at[at + side],
                    device_id=(row_at[dr], c), device_id_type=MESH,
                ))
        return held

    def start_rows(chunk, carry):
        for copy in row_copies(chunk):
            copy.start()
        return carry

    lax.fori_loop(0, chunks, start_rows, 0)

    modes[c, pl.ds(block, block)] = message[...]
    for copy in loads[4:]:
        copy.wait()
    for copy in vel_copies:
        copy.wait_recv()
    depth = rowof_ref.shape[1]
    offsets_at = jnp.zeros((tall, LANES), jnp.float32)
    lane = lax.broadcasted_iota(jnp.int32, (tall, LANES), 1)
    ext = lax.broadcasted_iota(jnp.int32, (tall, LANES), 0)
    for part in range(3):
        values = modes[c, part * block + 2 * group : (part + 1) * block, :][0:1]
        here = (lane == ext - HALO + rows_dev * (1 - part)) & (lane < rows_dev)
        offsets_at = offsets_at + jnp.where(here, values, 0.0)
    offset = jnp.dot(
        offsets_at, jnp.ones((LANES, depth), jnp.float32), preferred_element_type=jnp.float32
    )
    fine = lax.broadcasted_iota(jnp.int32, (tall, depth), 0)
    base = (fine // RATIO + (coarse_rows - 1)).astype(jnp.float32) + offset
    share = (fine % RATIO).astype(jnp.float32) / RATIO
    row_of = rowof_ref[0:1, :]
    near = jnp.where(jnp.abs(row_of - base) < 0.5, 1.0 - share, 0.0) + jnp.where(
        jnp.abs(row_of - base - 1.0) < 0.5, share, 0.0
    )
    for p in range(planes):
        blend_rows[p * tall : (p + 1) * tall, :] = (near * planes_ref[p : p + 1, :]).astype(
            jnp.bfloat16
        )
    scale = shift_ref[c]
    spectrum = jnp.concatenate(
        [modes[d] * scale[d : d + 1, :] for d in range(n_cols)], axis=-1
    )
    physical = jnp.dot(
        spectrum, transform_ref[...], precision=HIGHEST, preferred_element_type=jnp.float32
    )
    blend = blend_ref[...].astype(jnp.bfloat16)
    along = sum(
        jnp.dot(part, blend, preferred_element_type=jnp.float32)
        for part in reversed(parts_of(physical))
    )
    for m in range(2):
        picked = jnp.concatenate(
            [along[b * block + m * group : b * block + (m + 1) * group] for b in range(3)], axis=0
        )
        stack = list(parts_of(picked))
        short = depth - 9 * group
        if short:
            stack.append(jnp.zeros((short, picked.shape[1]), jnp.bfloat16))
        stacked = jnp.concatenate(stack, axis=0)
        for t in range(0, tiles, 2):
            wide = min(2, tiles - t)
            speed = jnp.dot(
                blend_rows[...], stacked[:, t * LANES : (t + wide) * LANES],
                preferred_element_type=jnp.float32,
            )
            for n in range(wide):
                speeds[m, t + n] = speed[:, n * LANES : (n + 1) * LANES].reshape(
                    planes, tall, LANES
                )

    for copy in strip_copies:
        copy.wait_recv()

    lane1 = lax.broadcasted_iota(jnp.int32, (SUB, LANES), 1)
    from_right = {k: lane1 < LANES - k for k in (1, 2)}
    from_left = {k: lane1 >= k for k in (1, 2)}
    halo_lane = lax.broadcasted_iota(jnp.int32, (tall, LANES), 1) < HALO

    def shifted(values, k):
        rolled = [pltpu.roll(v, (LANES - k) % LANES, 1) for v in values]
        if k > 0:
            return [
                jnp.where(from_right[k], rolled[t], rolled[(t + 1) % tiles]) for t in range(tiles)
            ]
        return [jnp.where(from_left[-k], rolled[t], rolled[t - 1]) for t in range(tiles)]

    def rows_of(ref, at, step=0):
        first = SUB + at + step
        return [ref[t, first : first + SUB, :] for t in range(tiles)]

    def tendency(ref, at):
        centre = rows_of(ref, at)
        ups, downs = rows_of(ref, at, 1), rows_of(ref, at, -1)
        ups2, downs2 = rows_of(ref, at, 2), rows_of(ref, at, -2)
        r1, l1, r2, l2 = (shifted(centre, k) for k in (1, -1, 2, -2))
        result = []
        for t in range(tiles):
            w = [coef[n, t, at : at + SUB, :] for n in range(7)]
            rows = w[0] * ups[t] + w[1] * downs[t] + w[5] * (ups2[t] - downs2[t])
            cols = w[2] * r1[t] + w[3] * l1[t] + w[6] * (r2[t] - l2[t])
            result.append((rows + cols) - w[4] * centre[t])
        return result

    def one_plane(p, carry):
        for array, (ref, work, gain) in enumerate(
            ((s_ref, field, None), (k_ref, kappa, 0.25 * TIME_STEP))
        ):
            def put(value):
                return value if gain is None else value * gain

            for t in range(own_tiles):
                at = slice(t * LANES, (t + 1) * LANES)
                work[t, SUB : SUB + HALO, :] = put(above[array, p, :, at])
                work[t, SUB + HALO : SUB + HALO + rows_dev, :] = put(ref[p, :, at])
                work[t, SUB + HALO + rows_dev : SUB + tall, :] = put(below[array, p, :, at])
            from_l = pltpu.roll(strips[0, array], lax.rem(2 * LANES - HALO * (p + 1), LANES), 1)
            from_r = pltpu.roll(strips[1, array], lax.rem(LANES - HALO * p, LANES), 1)
            work[own_tiles, SUB : SUB + tall, :] = put(jnp.where(halo_lane, from_r, from_l))

        for at in range(0, tall, SUB):
            centre = rows_of(kappa, at)
            ups, downs = rows_of(kappa, at, 1), rows_of(kappa, at, -1)
            rights, lefts = shifted(centre, 1), shifted(centre, -1)
            for t in range(tiles):
                u = speeds[0, t, p, at : at + SUB, :]
                v = speeds[1, t, p, at : at + SUB, :]
                u8, v8 = 8.0 * u, 8.0 * v
                east = centre[t] + ups[t] - u8
                west = centre[t] + downs[t] + u8
                north = centre[t] + rights[t] - v8
                south = centre[t] + lefts[t] + v8
                for n, value in enumerate(
                    (east, west, north, south, (east + west) + (north + south), u, v)
                ):
                    coef[n, t, at : at + SUB, :] = value

        for src, dst, span, gain in (
            (field, state_b, (0, tall), 1.0),
            (state_b, state_c, (4, tall - 4), 1.0),
            (state_c, state_d, (4, tall - 4), 2.0),
        ):
            for at in range(*span, SUB):
                slope = tendency(src, at)
                start = rows_of(field, at)
                for t in range(tiles):
                    dst[t, SUB + at : 2 * SUB + at, :] = start[t] + (
                        slope[t] if gain == 1.0 else gain * slope[t]
                    )
        for at in range(HALO, HALO + rows_dev, SUB):
            slope = tendency(state_d, at)
            a, b = rows_of(field, at), rows_of(state_b, at)
            e, g = rows_of(state_c, at), rows_of(state_d, at)
            for t in range(own_tiles):
                sums = (b[t] - a[t]) + 2.0 * e[t] + (g[t] + slope[t])
                o_ref[p, at - HALO : at - HALO + SUB, t * LANES : (t + 1) * LANES] = sums * (
                    1.0 / 3.0
                )
        return carry

    def one_chunk(chunk, carry):
        for copy in row_copies(chunk):
            copy.wait_recv()
        return lax.fori_loop(chunk * per_chunk, (chunk + 1) * per_chunk, one_plane, carry)

    lax.fori_loop(0, chunks, one_chunk, 0)

    def end_rows(chunk, carry):
        for copy in row_copies(chunk):
            copy.wait_send()
        return carry

    lax.fori_loop(0, chunks, end_rows, 0)
    for copy in vel_copies + strip_copies:
        copy.wait_send()


def solution(mesh):
    n_rows, n_cols = mesh.shape["rows"], mesh.shape["cols"]
    chunks = 8

    def per_device(scalar, diffusivity, vel_modes, offsets):
        planes, rows_dev, cols_dev = scalar.shape
        coarse, coarse_rows, modes_dev = vel_modes.shape
        consts = tables(n_cols, modes_dev, cols_dev, planes, coarse // 2, coarse_rows)
        tiles = cols_dev // LANES + 1
        tall = rows_dev + 2 * HALO
        group = -(-(coarse // 2 * coarse_rows) // 16) * 16
        block = 2 * group + SUB
        depth = consts[4].shape[1]
        partners = 3 * n_cols - 1
        work = pltpu.VMEM((tiles, tall + 2 * SUB, LANES), jnp.float32)
        dma = pltpu.SemaphoreType.DMA
        operands = (scalar, diffusivity, vel_modes, offsets.reshape(1, rows_dev), *consts)
        return pl.pallas_call(
            functools.partial(kernel, n_rows, n_cols, chunks),
            out_shape=jax.ShapeDtypeStruct(scalar.shape, jnp.float32),
            in_specs=[pl.BlockSpec(memory_space=pltpu.HBM)] * len(operands),
            out_specs=pl.BlockSpec(memory_space=pltpu.VMEM),
            scratch_shapes=[pltpu.VMEM(x.shape, x.dtype) for x in operands] + [
                dma((len(operands),)),
                pltpu.VMEM((block, 2 * modes_dev), jnp.float32),
                pltpu.VMEM((n_cols, 3 * block, 2 * modes_dev), jnp.float32),
                pltpu.VMEM((2, 2, rows_dev, LANES), jnp.float32),
                pltpu.VMEM((2, 2, tall, LANES), jnp.float32),
                pltpu.VMEM((2, planes, HALO, cols_dev), jnp.float32),
                pltpu.VMEM((2, planes, HALO, cols_dev), jnp.float32),
                pltpu.VMEM((planes * tall, depth), jnp.bfloat16),
                pltpu.VMEM((2, tiles, planes, tall, LANES), jnp.float32),
                work, work, work, work, work,
                pltpu.VMEM((7, tiles, tall, LANES), jnp.float32),
                dma((partners,)), dma((partners,)),
                dma((6,)), dma((6,)),
                dma((4 * chunks,)), dma((4 * chunks,)),
            ],
            compiler_params=pltpu.CompilerParams(
                collective_id=0, has_side_effects=True, vmem_limit_bytes=56 * 1024 * 1024
            ),
        )(*operands)

    return jax.shard_map(
        per_device,
        mesh=mesh,
        in_specs=(
            P(None, "rows", "cols"),
            P(None, "rows", "cols"),
            P(None, "rows", "cols"),
            P("rows"),
        ),
        out_specs=P(None, "rows", "cols"),
        check_vma=False,
    )
```

```python
import functools

import jax
import jax.numpy as jnp
import numpy as np
from jax import lax
from jax.experimental import pallas as pl
from jax.experimental.pallas import tpu as pltpu
from jax.sharding import PartitionSpec as P

TIME_STEP = 0.25
RATIO = 8
HALO = 8
LANES = 128
SUB = 8
MESH = pl.DeviceIdType.MESH
HIGHEST = lax.Precision.HIGHEST


def tables(count, modes_dev, cols_dev, planes, coarse_planes, coarse_rows):
    length = count * modes_dev
    coarse_cols = cols_dev // RATIO
    tiles = cols_dev // LANES + 1
    width = tiles * LANES

    def turn(product):
        return 2.0 * np.pi * (product % length) / length

    wavenum = np.arange(length).reshape(count, modes_dev)
    first = turn(np.arange(count)[:, None, None] * coarse_cols * wavenum[None])
    shift = np.concatenate([np.cos(first) + np.sin(first), np.cos(first) - np.sin(first)], axis=-1)
    shift = shift * (0.5 * TIME_STEP / 12.0)
    places = np.arange(coarse_cols + 3) - 1
    local = turn(wavenum[:, :, None] * places[None, None, :])
    local = np.concatenate([np.cos(local), np.sin(local)], axis=1).reshape(2 * length, -1)
    breadth = -(-local.shape[1] // LANES) * LANES
    transform = np.zeros((2 * length, breadth))
    transform[:, : local.shape[1]] = local
    lane = np.arange(width)
    fine = np.where(lane >= width - HALO, lane - width, np.minimum(lane, cols_dev + HALO - 1))
    col_blend = np.zeros((breadth, width))
    base = fine // RATIO + 1
    share = (fine % RATIO) / RATIO
    col_blend[base, lane] += 1.0 - share
    col_blend[base + 1, lane] += share
    group = -(-coarse_planes * coarse_rows // 16) * 16
    depth = -(-9 * group // LANES) * LANES
    plane_blend = np.zeros((planes, depth))
    row_of = np.full((SUB, depth), -100.0)
    plane = np.arange(planes)
    weights = np.zeros((planes, coarse_planes))
    for p in plane:
        weights[p, p // RATIO % coarse_planes] += 1.0 - (p % RATIO) / RATIO
        weights[p, (p // RATIO + 1) % coarse_planes] += (p % RATIO) / RATIO
    for part in range(3):
        for block in range(3):
            for q in range(coarse_planes):
                for a in range(coarse_rows):
                    at = (part * 3 + block) * group + q * coarse_rows + a
                    plane_blend[:, at] = weights[:, q]
                    row_of[:, at] = block * coarse_rows + a
    as_f32 = functools.partial(np.asarray, dtype=np.float32)
    return (
        as_f32(shift),
        as_f32(transform),
        as_f32(col_blend),
        as_f32(plane_blend),
        as_f32(row_of),
    )


def parts_of(value):
    high = value.astype(jnp.bfloat16)
    rest = value - high.astype(jnp.float32)
    middle = rest.astype(jnp.bfloat16)
    low = (rest - middle.astype(jnp.float32)).astype(jnp.bfloat16)
    return high, middle, low


def kernel(
    n_rows, n_cols, chunks,
    s_hbm, k_hbm, m_hbm, off_hbm, shift_hbm, transform_hbm, blend_hbm, planes_hbm, rowof_hbm,
    o_hbm,
    s_ref, k_ref, m_ref, off_ref, shift_ref, transform_ref, blend_ref, planes_ref, rowof_ref,
    load_sem, o_ref, store_sem,
    message, modes, packed, strips, above, below, blend_rows, speeds,
    field, kappa, state_b, state_c, state_d, coef,
    vel_send, vel_recv, strip_send, strip_recv, row_send, row_recv,
):
    planes, rows_dev, cols_dev = s_ref.shape
    own_tiles = cols_dev // LANES
    tiles = own_tiles + 1
    tall = rows_dev + 2 * HALO
    coarse = m_ref.shape[0]
    coarse_planes = coarse // 2
    coarse_rows = m_ref.shape[1]
    group = modes.shape[1] // 3 // 2 - SUB // 2
    block = 2 * group + SUB
    r = lax.axis_index("rows")
    c = lax.axis_index("cols")
    row_at = {-1: lax.rem(r + n_rows - 1, n_rows), 0: r, 1: lax.rem(r + 1, n_rows)}
    col_at = [c] + [lax.rem(c + d, n_cols) for d in range(1, n_cols)]
    left, right = col_at[n_cols - 1], col_at[1]

    loads = [
        pltpu.make_async_copy(src, dst, load_sem.at[i])
        for i, (src, dst) in enumerate((
            (m_hbm, m_ref), (off_hbm, off_ref), (s_hbm, s_ref), (k_hbm, k_ref),
            (shift_hbm, shift_ref), (transform_hbm, transform_ref), (blend_hbm, blend_ref),
            (planes_hbm, planes_ref), (rowof_hbm, rowof_ref),
        ))
    ]
    barrier = pltpu.get_barrier_semaphore()
    partners = [(dr, d) for d in range(n_cols) for dr in (-1, 0, 1) if (dr, d) != (0, 0)]
    for dr, d in partners:
        pl.semaphore_signal(barrier, inc=1, device_id=(row_at[dr], col_at[d]), device_id_type=MESH)

    for copy in loads:
        copy.start()
    message[...] = jnp.zeros_like(message)
    loads[0].wait()
    loads[1].wait()
    for part in range(coarse):
        at = part // coarse_planes * group + part % coarse_planes * coarse_rows
        once = m_ref[part]
        message[at : at + coarse_rows, :] = jnp.concatenate([once, once], axis=-1)
    message[2 * group :, 0:rows_dev] = jnp.broadcast_to(
        off_ref[...].astype(jnp.float32), (SUB, rows_dev)
    )
    pl.semaphore_wait(barrier, len(partners))

    def send(src, dst, sems, target):
        copy = pltpu.make_async_remote_copy(
            src_ref=src, dst_ref=dst, send_sem=sems[0], recv_sem=sems[1],
            device_id=target, device_id_type=MESH,
        )
        copy.start()
        return copy

    vel_copies = []
    for index, (dr, d) in enumerate(partners):
        vel_copies.append(send(
            message, modes.at[c, pl.ds((1 - dr) * block, block)],
            (vel_send.at[index], vel_recv.at[index]), (row_at[dr], col_at[d]),
        ))

    loads[2].wait()
    loads[3].wait()
    lane8 = lax.broadcasted_iota(jnp.int32, (rows_dev, LANES), 1)
    for side in range(2):
        for array, ref in enumerate((s_ref, k_ref)):
            total = jnp.zeros((rows_dev, LANES), jnp.float32)
            for p in range(planes):
                if side == 0:
                    edge = pltpu.roll(ref[p, :, 0:LANES], (HALO * p) % LANES, 1)
                else:
                    edge = pltpu.roll(ref[p, :, cols_dev - LANES :], (HALO * (p + 1)) % LANES, 1)
                total = jnp.where(lane8 // HALO == p, edge, total)
            packed[side, array] = total
    strip_copies = []
    for side, target in ((0, left), (1, right)):
        there = strips.at[1 - side]
        for index, (dr, first, extent, place) in enumerate((
            (0, 0, rows_dev, HALO),
            (-1, 0, HALO, HALO + rows_dev),
            (1, rows_dev - HALO, HALO, 0),
        )):
            at = side * 3 + index
            strip_copies.append(send(
                packed.at[side, :, pl.ds(first, extent)], there.at[:, pl.ds(place, extent)],
                (strip_send.at[at], strip_recv.at[at]), (row_at[dr], target),
            ))

    per_chunk = planes // chunks

    def row_copies(chunk):
        mine = pl.ds(chunk * per_chunk, per_chunk)
        held = []
        for array, ref in enumerate((s_ref, k_ref)):
            at = (chunk * 2 + array) * 2
            for side, (dr, first, there) in enumerate((
                (-1, 0, below), (1, rows_dev - HALO, above),
            )):
                held.append(pltpu.make_async_remote_copy(
                    src_ref=ref.at[mine, pl.ds(first, HALO)], dst_ref=there.at[array, mine],
                    send_sem=row_send.at[at + side], recv_sem=row_recv.at[at + side],
                    device_id=(row_at[dr], c), device_id_type=MESH,
                ))
        return held

    def start_rows(chunk, carry):
        for copy in row_copies(chunk):
            copy.start()
        return carry

    lax.fori_loop(0, chunks, start_rows, 0)

    modes[c, pl.ds(block, block)] = message[...]
    for copy in loads[4:]:
        copy.wait()
    for copy in vel_copies:
        copy.wait_recv()
    depth = rowof_ref.shape[1]
    offsets_at = jnp.zeros((tall, LANES), jnp.float32)
    lane = lax.broadcasted_iota(jnp.int32, (tall, LANES), 1)
    ext = lax.broadcasted_iota(jnp.int32, (tall, LANES), 0)
    for part in range(3):
        values = modes[c, part * block + 2 * group : (part + 1) * block, :][0:1]
        here = (lane == ext - HALO + rows_dev * (1 - part)) & (lane < rows_dev)
        offsets_at = offsets_at + jnp.where(here, values, 0.0)
    offset = jnp.dot(
        offsets_at, jnp.ones((LANES, depth), jnp.float32), preferred_element_type=jnp.float32
    )
    fine = lax.broadcasted_iota(jnp.int32, (tall, depth), 0)
    base = (fine // RATIO + (coarse_rows - 1)).astype(jnp.float32) + offset
    share = (fine % RATIO).astype(jnp.float32) / RATIO
    row_of = rowof_ref[0:1, :]
    near = jnp.where(jnp.abs(row_of - base) < 0.5, 1.0 - share, 0.0) + jnp.where(
        jnp.abs(row_of - base - 1.0) < 0.5, share, 0.0
    )
    for p in range(planes):
        blend_rows[p * tall : (p + 1) * tall, :] = (near * planes_ref[p : p + 1, :]).astype(
            jnp.bfloat16
        )
    scale = shift_ref[c]
    spectrum = jnp.concatenate(
        [modes[d] * scale[d : d + 1, :] for d in range(n_cols)], axis=-1
    )
    physical = jnp.dot(
        spectrum, transform_ref[...], precision=HIGHEST, preferred_element_type=jnp.float32
    )
    blend = blend_ref[...].astype(jnp.bfloat16)
    along = sum(
        jnp.dot(part, blend, preferred_element_type=jnp.float32)
        for part in reversed(parts_of(physical))
    )
    for m in range(2):
        picked = jnp.concatenate(
            [along[b * block + m * group : b * block + (m + 1) * group] for b in range(3)], axis=0
        )
        stack = list(parts_of(picked))
        short = depth - 9 * group
        if short:
            stack.append(jnp.zeros((short, picked.shape[1]), jnp.bfloat16))
        stacked = jnp.concatenate(stack, axis=0)
        for t in range(0, tiles, 2):
            wide = min(2, tiles - t)
            speed = jnp.dot(
                blend_rows[...], stacked[:, t * LANES : (t + wide) * LANES],
                preferred_element_type=jnp.float32,
            )
            for n in range(wide):
                speeds[m, t + n] = speed[:, n * LANES : (n + 1) * LANES].reshape(
                    planes, tall, LANES
                )

    for copy in strip_copies:
        copy.wait_recv()

    lane1 = lax.broadcasted_iota(jnp.int32, (SUB, LANES), 1)
    from_right = {k: lane1 < LANES - k for k in (1, 2)}
    from_left = {k: lane1 >= k for k in (1, 2)}
    halo_lane = lax.broadcasted_iota(jnp.int32, (tall, LANES), 1) < HALO

    def shifted(values, k):
        rolled = [pltpu.roll(v, (LANES - k) % LANES, 1) for v in values]
        if k > 0:
            return [
                jnp.where(from_right[k], rolled[t], rolled[(t + 1) % tiles]) for t in range(tiles)
            ]
        return [jnp.where(from_left[-k], rolled[t], rolled[t - 1]) for t in range(tiles)]

    def rows_of(ref, at, step=0):
        first = SUB + at + step
        return [ref[t, first : first + SUB, :] for t in range(tiles)]

    def tendency(ref, at):
        centre = rows_of(ref, at)
        ups, downs = rows_of(ref, at, 1), rows_of(ref, at, -1)
        ups2, downs2 = rows_of(ref, at, 2), rows_of(ref, at, -2)
        r1, l1, r2, l2 = (shifted(centre, k) for k in (1, -1, 2, -2))
        result = []
        for t in range(tiles):
            w = [coef[n, t, at : at + SUB, :] for n in range(7)]
            rows = w[0] * ups[t] + w[1] * downs[t] + w[5] * (ups2[t] - downs2[t])
            cols = w[2] * r1[t] + w[3] * l1[t] + w[6] * (r2[t] - l2[t])
            result.append((rows + cols) - w[4] * centre[t])
        return result

    def one_plane(p, carry):
        for array, (ref, work, gain) in enumerate(
            ((s_ref, field, None), (k_ref, kappa, 0.25 * TIME_STEP))
        ):
            def put(value):
                return value if gain is None else value * gain

            for t in range(own_tiles):
                at = slice(t * LANES, (t + 1) * LANES)
                work[t, SUB : SUB + HALO, :] = put(above[array, p, :, at])
                work[t, SUB + HALO : SUB + HALO + rows_dev, :] = put(ref[p, :, at])
                work[t, SUB + HALO + rows_dev : SUB + tall, :] = put(below[array, p, :, at])
            from_l = pltpu.roll(strips[0, array], lax.rem(2 * LANES - HALO * (p + 1), LANES), 1)
            from_r = pltpu.roll(strips[1, array], lax.rem(LANES - HALO * p, LANES), 1)
            work[own_tiles, SUB : SUB + tall, :] = put(jnp.where(halo_lane, from_r, from_l))

        for at in range(0, tall, SUB):
            centre = rows_of(kappa, at)
            ups, downs = rows_of(kappa, at, 1), rows_of(kappa, at, -1)
            rights, lefts = shifted(centre, 1), shifted(centre, -1)
            for t in range(tiles):
                u = speeds[0, t, p, at : at + SUB, :]
                v = speeds[1, t, p, at : at + SUB, :]
                u8, v8 = 8.0 * u, 8.0 * v
                east = centre[t] + ups[t] - u8
                west = centre[t] + downs[t] + u8
                north = centre[t] + rights[t] - v8
                south = centre[t] + lefts[t] + v8
                for n, value in enumerate(
                    (east, west, north, south, (east + west) + (north + south), u, v)
                ):
                    coef[n, t, at : at + SUB, :] = value

        for src, dst, span, gain in (
            (field, state_b, (0, tall), 1.0),
            (state_b, state_c, (4, tall - 4), 1.0),
            (state_c, state_d, (4, tall - 4), 2.0),
        ):
            for at in range(*span, SUB):
                slope = tendency(src, at)
                start = rows_of(field, at)
                for t in range(tiles):
                    dst[t, SUB + at : 2 * SUB + at, :] = start[t] + (
                        slope[t] if gain == 1.0 else gain * slope[t]
                    )
        for at in range(HALO, HALO + rows_dev, SUB):
            slope = tendency(state_d, at)
            a, b = rows_of(field, at), rows_of(state_b, at)
            e, g = rows_of(state_c, at), rows_of(state_d, at)
            for t in range(own_tiles):
                sums = (b[t] - a[t]) + 2.0 * e[t] + (g[t] + slope[t])
                o_ref[p, at - HALO : at - HALO + SUB, t * LANES : (t + 1) * LANES] = sums * (
                    1.0 / 3.0
                )
        return carry

    def store(chunk):
        done = pl.ds(chunk * per_chunk, per_chunk)
        return pltpu.make_async_copy(o_ref.at[done], o_hbm.at[done], store_sem.at[chunk])

    def one_chunk(chunk, carry):
        for copy in row_copies(chunk):
            copy.wait_recv()
        lax.fori_loop(chunk * per_chunk, (chunk + 1) * per_chunk, one_plane, 0)
        store(chunk).start()
        return carry

    lax.fori_loop(0, chunks, one_chunk, 0)

    def end_rows(chunk, carry):
        for copy in row_copies(chunk):
            copy.wait_send()
        store(chunk).wait()
        return carry

    lax.fori_loop(0, chunks, end_rows, 0)
    for copy in vel_copies + strip_copies:
        copy.wait_send()


def solution(mesh):
    n_rows, n_cols = mesh.shape["rows"], mesh.shape["cols"]
    chunks = 8

    def per_device(scalar, diffusivity, vel_modes, offsets):
        planes, rows_dev, cols_dev = scalar.shape
        coarse, coarse_rows, modes_dev = vel_modes.shape
        consts = tables(n_cols, modes_dev, cols_dev, planes, coarse // 2, coarse_rows)
        tiles = cols_dev // LANES + 1
        tall = rows_dev + 2 * HALO
        group = -(-(coarse // 2 * coarse_rows) // 16) * 16
        block = 2 * group + SUB
        depth = consts[4].shape[1]
        partners = 3 * n_cols - 1
        work = pltpu.VMEM((tiles, tall + 2 * SUB, LANES), jnp.float32)
        dma = pltpu.SemaphoreType.DMA
        operands = (scalar, diffusivity, vel_modes, offsets.reshape(1, rows_dev), *consts)
        return pl.pallas_call(
            functools.partial(kernel, n_rows, n_cols, chunks),
            out_shape=jax.ShapeDtypeStruct(scalar.shape, jnp.float32),
            in_specs=[pl.BlockSpec(memory_space=pltpu.HBM)] * len(operands),
            out_specs=pl.BlockSpec(memory_space=pl.ANY),
            scratch_shapes=[pltpu.VMEM(x.shape, x.dtype) for x in operands] + [
                dma((len(operands),)), pltpu.VMEM(scalar.shape, jnp.float32), dma((chunks,)),
                pltpu.VMEM((block, 2 * modes_dev), jnp.float32),
                pltpu.VMEM((n_cols, 3 * block, 2 * modes_dev), jnp.float32),
                pltpu.VMEM((2, 2, rows_dev, LANES), jnp.float32),
                pltpu.VMEM((2, 2, tall, LANES), jnp.float32),
                pltpu.VMEM((2, planes, HALO, cols_dev), jnp.float32),
                pltpu.VMEM((2, planes, HALO, cols_dev), jnp.float32),
                pltpu.VMEM((planes * tall, depth), jnp.bfloat16),
                pltpu.VMEM((2, tiles, planes, tall, LANES), jnp.float32),
                work, work, work, work, work,
                pltpu.VMEM((7, tiles, tall, LANES), jnp.float32),
                dma((partners,)), dma((partners,)),
                dma((6,)), dma((6,)),
                dma((4 * chunks,)), dma((4 * chunks,)),
            ],
            compiler_params=pltpu.CompilerParams(
                collective_id=0, has_side_effects=True, vmem_limit_bytes=56 * 1024 * 1024
            ),
        )(*operands)

    return jax.shard_map(
        per_device,
        mesh=mesh,
        in_specs=(
            P(None, "rows", "cols"),
            P(None, "rows", "cols"),
            P(None, "rows", "cols"),
            P("rows"),
        ),
        out_specs=P(None, "rows", "cols"),
        check_vma=False,
    )
```

```python
import functools

import jax
import jax.numpy as jnp
import numpy as np
from jax import lax
from jax.experimental import pallas as pl
from jax.experimental.pallas import tpu as pltpu
from jax.sharding import PartitionSpec as P

TIME_STEP = 0.25
RATIO = 8
HALO = 8
LANES = 128
SUB = 8
MESH = pl.DeviceIdType.MESH
HIGHEST = lax.Precision.HIGHEST


def tables(count, modes_dev, cols_dev, planes, coarse_planes, coarse_rows):
    length = count * modes_dev
    coarse_cols = cols_dev // RATIO
    tiles = cols_dev // LANES + 1
    width = tiles * LANES

    def turn(product):
        return 2.0 * np.pi * (product % length) / length

    wavenum = np.arange(length).reshape(count, modes_dev)
    first = turn(np.arange(count)[:, None, None] * coarse_cols * wavenum[None])
    shift = np.concatenate([np.cos(first) + np.sin(first), np.cos(first) - np.sin(first)], axis=-1)
    shift = shift * (0.5 * TIME_STEP / 12.0)
    places = np.arange(coarse_cols + 3) - 1
    local = turn(wavenum[:, :, None] * places[None, None, :])
    local = np.concatenate([np.cos(local), np.sin(local)], axis=1).reshape(2 * length, -1)
    breadth = -(-local.shape[1] // LANES) * LANES
    transform = np.zeros((2 * length, breadth))
    transform[:, : local.shape[1]] = local
    lane = np.arange(width)
    fine = np.where(lane >= width - HALO, lane - width, np.minimum(lane, cols_dev + HALO - 1))
    col_blend = np.zeros((breadth, width))
    base = fine // RATIO + 1
    share = (fine % RATIO) / RATIO
    col_blend[base, lane] += 1.0 - share
    col_blend[base + 1, lane] += share
    group = -(-coarse_planes * coarse_rows // 16) * 16
    depth = -(-9 * group // LANES) * LANES
    plane_blend = np.zeros((planes, depth))
    row_of = np.full((SUB, depth), -100.0)
    plane = np.arange(planes)
    weights = np.zeros((planes, coarse_planes))
    for p in plane:
        weights[p, p // RATIO % coarse_planes] += 1.0 - (p % RATIO) / RATIO
        weights[p, (p // RATIO + 1) % coarse_planes] += (p % RATIO) / RATIO
    for part in range(3):
        for block in range(3):
            for q in range(coarse_planes):
                for a in range(coarse_rows):
                    at = (part * 3 + block) * group + q * coarse_rows + a
                    plane_blend[:, at] = weights[:, q]
                    row_of[:, at] = block * coarse_rows + a
    as_f32 = functools.partial(np.asarray, dtype=np.float32)
    return (
        as_f32(shift),
        as_f32(transform),
        as_f32(col_blend),
        as_f32(plane_blend),
        as_f32(row_of),
    )


def parts_of(value):
    high = value.astype(jnp.bfloat16)
    rest = value - high.astype(jnp.float32)
    middle = rest.astype(jnp.bfloat16)
    low = (rest - middle.astype(jnp.float32)).astype(jnp.bfloat16)
    return high, middle, low


def kernel(
    n_rows, n_cols, chunks,
    s_hbm, k_hbm, m_hbm, off_hbm, shift_hbm, transform_hbm, blend_hbm, planes_hbm, rowof_hbm,
    o_hbm,
    s_ref, k_ref, m_ref, off_ref, shift_ref, transform_ref, blend_ref, planes_ref, rowof_ref,
    load_sem, o_ref, store_sem,
    message, modes, packed, strips, above, below, blend_rows, speeds,
    field, kappa, state_b, state_c, state_d, coef,
    vel_send, vel_recv, strip_send, strip_recv, row_send, row_recv,
):
    planes, rows_dev, cols_dev = s_ref.shape
    own_tiles = cols_dev // LANES
    tiles = own_tiles + 1
    tall = rows_dev + 2 * HALO
    coarse = m_ref.shape[0]
    coarse_planes = coarse // 2
    coarse_rows = m_ref.shape[1]
    group = modes.shape[1] // 3 // 2 - SUB // 2
    block = 2 * group + SUB
    r = lax.axis_index("rows")
    c = lax.axis_index("cols")
    row_at = {-1: lax.rem(r + n_rows - 1, n_rows), 0: r, 1: lax.rem(r + 1, n_rows)}
    col_at = [c] + [lax.rem(c + d, n_cols) for d in range(1, n_cols)]
    left, right = col_at[n_cols - 1], col_at[1]

    loads = [
        pltpu.make_async_copy(src, dst, load_sem.at[i])
        for i, (src, dst) in enumerate((
            (m_hbm, m_ref), (off_hbm, off_ref), (s_hbm, s_ref), (k_hbm, k_ref),
            (shift_hbm, shift_ref), (transform_hbm, transform_ref), (blend_hbm, blend_ref),
            (planes_hbm, planes_ref), (rowof_hbm, rowof_ref),
        ))
    ]
    barrier = pltpu.get_barrier_semaphore()
    partners = [(dr, d) for d in range(n_cols) for dr in (-1, 0, 1) if (dr, d) != (0, 0)]
    for dr, d in partners:
        pl.semaphore_signal(barrier, inc=1, device_id=(row_at[dr], col_at[d]), device_id_type=MESH)

    for copy in loads:
        copy.start()
    message[...] = jnp.zeros_like(message)
    loads[0].wait()
    loads[1].wait()
    for part in range(coarse):
        at = part // coarse_planes * group + part % coarse_planes * coarse_rows
        once = m_ref[part]
        message[at : at + coarse_rows, :] = jnp.concatenate([once, once], axis=-1)
    message[2 * group :, 0:rows_dev] = jnp.broadcast_to(
        off_ref[...].astype(jnp.float32), (SUB, rows_dev)
    )
    pl.semaphore_wait(barrier, len(partners))

    def send(src, dst, sems, target):
        copy = pltpu.make_async_remote_copy(
            src_ref=src, dst_ref=dst, send_sem=sems[0], recv_sem=sems[1],
            device_id=target, device_id_type=MESH,
        )
        copy.start()
        return copy

    vel_copies = []
    for index, (dr, d) in enumerate(partners):
        vel_copies.append(send(
            message, modes.at[c, pl.ds((1 - dr) * block, block)],
            (vel_send.at[index], vel_recv.at[index]), (row_at[dr], col_at[d]),
        ))

    loads[2].wait()
    loads[3].wait()
    lane8 = lax.broadcasted_iota(jnp.int32, (rows_dev, LANES), 1)
    for side in range(2):
        for array, ref in enumerate((s_ref, k_ref)):
            total = jnp.zeros((rows_dev, LANES), jnp.float32)
            for p in range(planes):
                if side == 0:
                    edge = pltpu.roll(ref[p, :, 0:LANES], (HALO * p) % LANES, 1)
                else:
                    edge = pltpu.roll(ref[p, :, cols_dev - LANES :], (HALO * (p + 1)) % LANES, 1)
                total = jnp.where(lane8 // HALO == p, edge, total)
            packed[side, array] = total
    strip_copies = []
    for side, target in ((0, left), (1, right)):
        there = strips.at[1 - side]
        for index, (dr, first, extent, place) in enumerate((
            (0, 0, rows_dev, HALO),
            (-1, 0, HALO, HALO + rows_dev),
            (1, rows_dev - HALO, HALO, 0),
        )):
            at = side * 3 + index
            strip_copies.append(send(
                packed.at[side, :, pl.ds(first, extent)], there.at[:, pl.ds(place, extent)],
                (strip_send.at[at], strip_recv.at[at]), (row_at[dr], target),
            ))

    per_chunk = planes // chunks

    def row_copies(chunk):
        mine = pl.ds(chunk * per_chunk, per_chunk)
        held = []
        for array, ref in enumerate((s_ref, k_ref)):
            at = (chunk * 2 + array) * 2
            for side, (dr, first, there) in enumerate((
                (-1, 0, below), (1, rows_dev - HALO, above),
            )):
                held.append(pltpu.make_async_remote_copy(
                    src_ref=ref.at[mine, pl.ds(first, HALO)], dst_ref=there.at[array, mine],
                    send_sem=row_send.at[at + side], recv_sem=row_recv.at[at + side],
                    device_id=(row_at[dr], c), device_id_type=MESH,
                ))
        return held

    def start_rows(chunk, carry):
        for copy in row_copies(chunk):
            copy.start()
        return carry

    lax.fori_loop(0, chunks, start_rows, 0)

    modes[c, pl.ds(block, block)] = message[...]
    for copy in loads[4:]:
        copy.wait()
    for copy in vel_copies:
        copy.wait_recv()
    depth = rowof_ref.shape[1]
    offsets_at = jnp.zeros((tall, LANES), jnp.float32)
    lane = lax.broadcasted_iota(jnp.int32, (tall, LANES), 1)
    ext = lax.broadcasted_iota(jnp.int32, (tall, LANES), 0)
    for part in range(3):
        values = modes[c, part * block + 2 * group : (part + 1) * block, :][0:1]
        here = (lane == ext - HALO + rows_dev * (1 - part)) & (lane < rows_dev)
        offsets_at = offsets_at + jnp.where(here, values, 0.0)
    offset = jnp.dot(
        offsets_at, jnp.ones((LANES, depth), jnp.float32), preferred_element_type=jnp.float32
    )
    fine = lax.broadcasted_iota(jnp.int32, (tall, depth), 0)
    base = (fine // RATIO + (coarse_rows - 1)).astype(jnp.float32) + offset
    share = (fine % RATIO).astype(jnp.float32) / RATIO
    row_of = rowof_ref[0:1, :]
    near = jnp.where(jnp.abs(row_of - base) < 0.5, 1.0 - share, 0.0) + jnp.where(
        jnp.abs(row_of - base - 1.0) < 0.5, share, 0.0
    )
    for p in range(planes):
        blend_rows[p * tall : (p + 1) * tall, :] = (near * planes_ref[p : p + 1, :]).astype(
            jnp.bfloat16
        )
    scale = shift_ref[c]
    spectrum = jnp.concatenate(
        [modes[d] * scale[d : d + 1, :] for d in range(n_cols)], axis=-1
    )
    physical = jnp.dot(
        spectrum, transform_ref[...], precision=HIGHEST, preferred_element_type=jnp.float32
    )
    blend = blend_ref[...].astype(jnp.bfloat16)
    along = sum(
        jnp.dot(part, blend, preferred_element_type=jnp.float32)
        for part in reversed(parts_of(physical))
    )
    for m in range(2):
        picked = jnp.concatenate(
            [along[b * block + m * group : b * block + (m + 1) * group] for b in range(3)], axis=0
        )
        stack = list(parts_of(picked))
        short = depth - 9 * group
        if short:
            stack.append(jnp.zeros((short, picked.shape[1]), jnp.bfloat16))
        stacked = jnp.concatenate(stack, axis=0)
        for t in range(0, tiles, 2):
            wide = min(2, tiles - t)
            speed = jnp.dot(
                blend_rows[...], stacked[:, t * LANES : (t + wide) * LANES],
                preferred_element_type=jnp.float32,
            )
            for n in range(wide):
                speeds[m, t + n] = speed[:, n * LANES : (n + 1) * LANES].reshape(
                    planes, tall, LANES
                )

    for copy in strip_copies:
        copy.wait_recv()

    lane1 = lax.broadcasted_iota(jnp.int32, (SUB, LANES), 1)
    from_right = {k: lane1 < LANES - k for k in (1, 2)}
    from_left = {k: lane1 >= k for k in (1, 2)}
    halo_lane = lax.broadcasted_iota(jnp.int32, (tall, LANES), 1) < HALO

    def shifted(values, k):
        rolled = [pltpu.roll(v, (LANES - k) % LANES, 1) for v in values]
        if k > 0:
            return [
                jnp.where(from_right[k], rolled[t], rolled[(t + 1) % tiles]) for t in range(tiles)
            ]
        return [jnp.where(from_left[-k], rolled[t], rolled[t - 1]) for t in range(tiles)]

    def rows_of(ref, at, step=0):
        first = SUB + at + step
        return [ref[t, first : first + SUB, :] for t in range(tiles)]

    def tendency(ref, at):
        centre = rows_of(ref, at)
        ups, downs = rows_of(ref, at, 1), rows_of(ref, at, -1)
        ups2, downs2 = rows_of(ref, at, 2), rows_of(ref, at, -2)
        r1, l1, r2, l2 = (shifted(centre, k) for k in (1, -1, 2, -2))
        result = []
        for t in range(tiles):
            w = [coef[n, t, at : at + SUB, :] for n in range(7)]
            rows = w[0] * ups[t] + w[1] * downs[t] + w[5] * (ups2[t] - downs2[t])
            cols = w[2] * r1[t] + w[3] * l1[t] + w[6] * (r2[t] - l2[t])
            result.append((rows + cols) - w[4] * centre[t])
        return result

    def one_plane(p, carry):
        for array, (ref, work, gain) in enumerate(
            ((s_ref, field, None), (k_ref, kappa, 0.25 * TIME_STEP))
        ):
            def put(value):
                return value if gain is None else value * gain

            for t in range(own_tiles):
                at = slice(t * LANES, (t + 1) * LANES)
                work[t, SUB : SUB + HALO, :] = put(above[array, p, :, at])
                work[t, SUB + HALO : SUB + HALO + rows_dev, :] = put(ref[p, :, at])
                work[t, SUB + HALO + rows_dev : SUB + tall, :] = put(below[array, p, :, at])
            from_l = pltpu.roll(strips[0, array], lax.rem(2 * LANES - HALO * (p + 1), LANES), 1)
            from_r = pltpu.roll(strips[1, array], lax.rem(LANES - HALO * p, LANES), 1)
            work[own_tiles, SUB : SUB + tall, :] = put(jnp.where(halo_lane, from_r, from_l))

        for at in range(0, tall, SUB):
            centre = rows_of(kappa, at)
            ups, downs = rows_of(kappa, at, 1), rows_of(kappa, at, -1)
            rights, lefts = shifted(centre, 1), shifted(centre, -1)
            for t in range(tiles):
                u = speeds[0, t, p, at : at + SUB, :]
                v = speeds[1, t, p, at : at + SUB, :]
                u8, v8 = 8.0 * u, 8.0 * v
                east = centre[t] + ups[t] - u8
                west = centre[t] + downs[t] + u8
                north = centre[t] + rights[t] - v8
                south = centre[t] + lefts[t] + v8
                for n, value in enumerate(
                    (east, west, north, south, (east + west) + (north + south), u, v)
                ):
                    coef[n, t, at : at + SUB, :] = value

        for src, dst, span, gain in (
            (field, state_b, (0, tall), 1.0),
            (state_b, state_c, (4, tall - 4), 1.0),
            (state_c, state_d, (4, tall - 4), 2.0),
        ):
            for at in range(*span, SUB):
                slope = tendency(src, at)
                start = rows_of(field, at)
                for t in range(tiles):
                    dst[t, SUB + at : 2 * SUB + at, :] = start[t] + (
                        slope[t] if gain == 1.0 else gain * slope[t]
                    )
        for at in range(HALO, HALO + rows_dev, SUB):
            slope = tendency(state_d, at)
            a, b = rows_of(field, at), rows_of(state_b, at)
            e, g = rows_of(state_c, at), rows_of(state_d, at)
            for t in range(own_tiles):
                sums = (b[t] - a[t]) + 2.0 * e[t] + (g[t] + slope[t])
                o_ref[p, at - HALO : at - HALO + SUB, t * LANES : (t + 1) * LANES] = sums * (
                    1.0 / 3.0
                )
        return carry

    def store(chunk):
        done = pl.ds(chunk * per_chunk, per_chunk)
        return pltpu.make_async_copy(o_ref.at[done], o_hbm.at[done], store_sem.at[chunk])

    def one_chunk(chunk, carry):
        for copy in row_copies(chunk):
            copy.wait_recv()
        lax.fori_loop(chunk * per_chunk, (chunk + 1) * per_chunk, one_plane, 0)
        store(chunk).start()
        return carry

    lax.fori_loop(0, chunks, one_chunk, 0)

    def end_rows(chunk, carry):
        for copy in row_copies(chunk):
            copy.wait_send()
        store(chunk).wait()
        return carry

    lax.fori_loop(0, chunks, end_rows, 0)
    for copy in vel_copies + strip_copies:
        copy.wait_send()


def solution(mesh):
    n_rows, n_cols = mesh.shape["rows"], mesh.shape["cols"]
    chunks = 16

    def per_device(scalar, diffusivity, vel_modes, offsets):
        planes, rows_dev, cols_dev = scalar.shape
        coarse, coarse_rows, modes_dev = vel_modes.shape
        consts = tables(n_cols, modes_dev, cols_dev, planes, coarse // 2, coarse_rows)
        tiles = cols_dev // LANES + 1
        tall = rows_dev + 2 * HALO
        group = -(-(coarse // 2 * coarse_rows) // 16) * 16
        block = 2 * group + SUB
        depth = consts[4].shape[1]
        partners = 3 * n_cols - 1
        work = pltpu.VMEM((tiles, tall + 2 * SUB, LANES), jnp.float32)
        dma = pltpu.SemaphoreType.DMA
        operands = (scalar, diffusivity, vel_modes, offsets.reshape(1, rows_dev), *consts)
        return pl.pallas_call(
            functools.partial(kernel, n_rows, n_cols, chunks),
            out_shape=jax.ShapeDtypeStruct(scalar.shape, jnp.float32),
            in_specs=[pl.BlockSpec(memory_space=pltpu.HBM)] * len(operands),
            out_specs=pl.BlockSpec(memory_space=pl.ANY),
            scratch_shapes=[pltpu.VMEM(x.shape, x.dtype) for x in operands] + [
                dma((len(operands),)), pltpu.VMEM(scalar.shape, jnp.float32), dma((chunks,)),
                pltpu.VMEM((block, 2 * modes_dev), jnp.float32),
                pltpu.VMEM((n_cols, 3 * block, 2 * modes_dev), jnp.float32),
                pltpu.VMEM((2, 2, rows_dev, LANES), jnp.float32),
                pltpu.VMEM((2, 2, tall, LANES), jnp.float32),
                pltpu.VMEM((2, planes, HALO, cols_dev), jnp.float32),
                pltpu.VMEM((2, planes, HALO, cols_dev), jnp.float32),
                pltpu.VMEM((planes * tall, depth), jnp.bfloat16),
                pltpu.VMEM((2, tiles, planes, tall, LANES), jnp.float32),
                work, work, work, work, work,
                pltpu.VMEM((7, tiles, tall, LANES), jnp.float32),
                dma((partners,)), dma((partners,)),
                dma((6,)), dma((6,)),
                dma((4 * chunks,)), dma((4 * chunks,)),
            ],
            compiler_params=pltpu.CompilerParams(
                collective_id=0, has_side_effects=True, vmem_limit_bytes=56 * 1024 * 1024
            ),
        )(*operands)

    return jax.shard_map(
        per_device,
        mesh=mesh,
        in_specs=(
            P(None, "rows", "cols"),
            P(None, "rows", "cols"),
            P(None, "rows", "cols"),
            P("rows"),
        ),
        out_specs=P(None, "rows", "cols"),
        check_vma=False,
    )
```
